32 devices in a mesh: gx: 8 (over z, core), fam: 4 (over y, x).
Axes of the slice: x: 2, y: 2, z: 4, core: 2. Of those that a mesh axis runs over, the one named last changes fastest.
Arguments:
- labels: int32 [1, 512, 512], P(None, 'gx'), may hold values from 0 to 2047, as said below
- family_of_grain: int32 [2048], replicated, may hold values from 0 to 255
Outputs:
- distance: float32 [256, 1, 512, 512], P('fam', None, 'gx')
The draws below stay inside these ranges and needn't reach their ends.
Inputs may be any that keep to these rules, and one draw needn't show every extreme that they name: `labels`: cells lie mostly in square grains of 32 x 32 cells; about a quarter of the cells carry some other grain.
All inputs are finite; a program needn't handle non-finite values.
Results may differ from the reference program's by a relative error of at most 0.0019.
Values may be sent and summed in bfloat16 or wider, within the bound.
A program may use at most 128 MiB of HBM per device.

```python
import jax
import jax.numpy as jnp
from jax import lax

F = 256
NX = 512
NY = 512
NZ = 1
GRAINS = 2048
BLOCK = 32
WIDTH = 2
SWEEPS = 3


def draw_labels(key, part):
    first = jax.random.fold_in(key, 11)
    second = jax.random.fold_in(key, 12)
    third = jax.random.fold_in(key, 13)
    coarse = jax.random.randint(first, (NZ, NX // BLOCK, NY // BLOCK), 0, GRAINS)
    coarse = jnp.repeat(jnp.repeat(coarse, BLOCK, axis=1), BLOCK, axis=2)
    flip = jax.random.randint(second, (NZ, NX, NY), 0, 4) == 0
    other = jax.random.randint(third, (NZ, NX, NY), 0, GRAINS)
    return jnp.where(flip, other, coarse).astype(jnp.int32)


def set_ends(result, rng, least, high):
    spot = [jax.random.randint(jax.random.fold_in(rng, axis), (), 0, length) for axis, length in enumerate(result.shape)]
    main_axis = result.shape.index(max(result.shape))
    beside = spot[:main_axis] + [(spot[main_axis] + 1) % result.shape[main_axis]] + spot[main_axis + 1:]
    return result.at[tuple(spot)].set(least).at[tuple(beside)].set(high)


def setup_inputs(seed: int = 0) -> dict:
    key_of = jax.random.split(jax.random.key(seed), 3)
    return {
        "labels": draw_labels(jax.random.fold_in(key_of[2], 71), 0),
        "family_of_grain": set_ends(jax.random.randint(key_of[1], (GRAINS,), 0, F), jax.random.fold_in(key_of[1], 1), 0, F - 1).astype(jnp.int32),
    }


fidelity = 0.25
scale_factor = 8.0
step_size = 0.5

def cas_table(count):
    idx = jnp.arange(count).astype(jnp.float32)
    angle = 2.0 * jnp.pi * jnp.outer(idx, idx) / count
    return (jnp.cos(angle) + jnp.sin(angle)).astype(jnp.bfloat16)

def gauss_table(count):
    freq = jnp.arange(count)
    mirror = jnp.minimum(freq, count - freq).astype(jnp.float32)
    sigma = WIDTH / 2.0
    return jnp.exp(-2.0 * jnp.pi ** 2 * sigma ** 2 * mirror ** 2 / (count * count))

def godunov(ext, sign):
    centre = ext[:, :, 1:-1]
    pairs = [(centre - ext[:, :, :-2], ext[:, :, 2:] - centre), (centre - jnp.roll(centre, 1, 3), jnp.roll(centre, -1, 3) - centre), (centre - jnp.roll(centre, 1, 1), jnp.roll(centre, -1, 1) - centre)]
    plus = jnp.zeros_like(centre)
    minus = jnp.zeros_like(centre)
    for back, fore in pairs:
        plus = plus + jnp.maximum(jnp.maximum(back, 0.0) ** 2, jnp.minimum(fore, 0.0) ** 2)
        minus = minus + jnp.maximum(jnp.minimum(back, 0.0) ** 2, jnp.maximum(fore, 0.0) ** 2)
    grad = jnp.sqrt(jnp.where(sign > 0, plus, minus))
    return centre - step_size * sign * (grad - 1.0)

def reference(labels, family_of_grain):
    group = 8
    owner = jnp.take(family_of_grain, labels, axis=0)
    cas_x = cas_table(NX).astype(jnp.float32)
    cas_y = cas_table(NY).astype(jnp.float32)
    gauss_x = gauss_table(NX)
    gauss_y = gauss_table(NY)

    def smooth_group(start):
        ids = start + jnp.arange(group)
        chi = (owner[None] == ids[:, None, None, None]).astype(jnp.bfloat16)
        spec_y = (jnp.einsum('fzxy,yk->fzxk', chi.astype(jnp.float32), cas_y) * gauss_y).astype(jnp.bfloat16)
        spec_xy = (jnp.einsum('fzxk,xq->fzqk', spec_y.astype(jnp.float32), cas_x) * gauss_x[None, None, :, None]).astype(jnp.bfloat16)
        back_x = (jnp.einsum('fzqk,qx->fzxk', spec_xy.astype(jnp.float32), cas_x) * (1.0 / NX)).astype(jnp.bfloat16)
        smooth = jnp.einsum('fzxk,ky->fzxy', back_x.astype(jnp.float32), cas_y) * (1.0 / NY)
        return smooth + fidelity * chi.astype(jnp.float32)

    def first_pass(carry, start):
        high, second = carry
        u = smooth_group(start)
        for j in range(group):
            second = jnp.maximum(jnp.minimum(high, u[j]), second)
            high = jnp.maximum(high, u[j])
        return ((high, second), u)
    lowest = jnp.full((NZ, NX, NY), -1e+30, jnp.float32)
    starts = (jnp.arange(F // group) * group).astype(jnp.int32)
    (top1, top2), u_all = lax.scan(first_pass, (lowest, lowest), starts)

    def finish(u):
        phi0 = scale_factor * (u - jnp.where(u >= top1, top2, top1))
        sign = phi0 / jnp.sqrt(phi0 * phi0 + 1.0)
        phi = phi0
        for sweep in range(SWEEPS):
            ext = jnp.pad(phi, ((0, 0), (0, 0), (1, 1), (0, 0)), mode='wrap')
            phi = godunov(ext, sign)
        return phi
    out = lax.map(finish, u_all)
    return out.reshape(F, NZ, NX, NY)
```

```python
import functools

import jax
import jax.numpy as jnp
import ml_dtypes
import numpy as np
from jax import lax
from jax.experimental import pallas as pl
from jax.experimental.pallas import tpu as pltpu
from jax.sharding import PartitionSpec as P

F = 256
WIDTH = 2
SWEEPS = 3
HALO = 8
LANES = 128
BIG = -1e30
MESH = pl.DeviceIdType.MESH

fidelity = 0.25
scale_factor = 8.0
step_size = 0.5


def smoothing(count):
    idx = np.arange(count).astype(np.float32)
    angle = (np.float32(2.0 * np.pi) * np.outer(idx, idx)) / np.float32(count)
    cas = (np.cos(angle) + np.sin(angle)).astype(ml_dtypes.bfloat16).astype(np.float64)
    freq = np.arange(count)
    mirror = np.minimum(freq, count - freq).astype(np.float64)
    sigma = WIDTH / 2.0
    gauss = np.exp(-2.0 * np.pi**2 * sigma**2 * mirror**2 / (count * count))
    full = (cas * gauss) @ cas.T / count
    high = full.astype(ml_dtypes.bfloat16)
    low = (full - high.astype(np.float64)).astype(ml_dtypes.bfloat16)
    return high, low


def ring_rows(x_local, count, parts):
    rows = x_local + HALO
    out = []
    for part in range(parts):
        r = np.arange(rows)
        x = part * x_local + np.where(r < x_local + HALO // 2, r, r - rows)
        out.append(x % count)
    return np.stack(out)


def owner_kernel(labels_ref, table_ref, out_ref):
    rows, cols = labels_ref.shape
    n_table = table_ref.shape[0]
    for c in range(cols // LANES):
        lab = labels_ref[:, c * LANES : (c + 1) * LANES]
        page = lab // LANES
        lane = lab % LANES
        acc = jnp.zeros((rows, LANES), jnp.int32)
        for k in range(n_table):
            row = jnp.broadcast_to(table_ref[k : k + 1, :], (rows, LANES))
            got = jnp.take_along_axis(row, lane, axis=1)
            acc = jnp.where(page == k, got, acc)
        out_ref[:, c * LANES : (c + 1) * LANES] = acc.astype(jnp.float32).astype(out_ref.dtype)


def owners(labels, table):
    return pl.pallas_call(
        owner_kernel,
        out_shape=jax.ShapeDtypeStruct(labels.shape, jnp.bfloat16),
        name="owner_lookup",
    )(labels, table)


def gather_kernel(axis, size, x_ref, out_ref, send_sem, recv_sem, local_sem):
    me = lax.axis_index(axis)
    barrier = pltpu.get_barrier_semaphore()
    for k in range(1, size):
        pl.semaphore_signal(
            barrier, inc=1, device_id={axis: lax.rem(me + k, size)}, device_id_type=MESH
        )
    local = pltpu.make_async_copy(x_ref, out_ref.at[me], local_sem)
    local.start()
    pl.semaphore_wait(barrier, size - 1)
    copies = []
    for k in range(1, size):
        copy = pltpu.make_async_remote_copy(
            src_ref=x_ref,
            dst_ref=out_ref.at[me],
            send_sem=send_sem.at[k - 1],
            recv_sem=recv_sem.at[k - 1],
            device_id={axis: lax.rem(me + k, size)},
            device_id_type=MESH,
        )
        copy.start()
        copies.append(copy)
    local.wait()
    for copy in copies:
        copy.wait()


def gathered(x, axis, size, collective_id):
    return pl.pallas_call(
        functools.partial(gather_kernel, axis, size),
        out_shape=jax.ShapeDtypeStruct((size, *x.shape), x.dtype),
        in_specs=[pl.BlockSpec(memory_space=pltpu.VMEM)],
        out_specs=pl.BlockSpec(memory_space=pltpu.VMEM),
        scratch_shapes=[
            pltpu.SemaphoreType.DMA((size - 1,)),
            pltpu.SemaphoreType.DMA((size - 1,)),
            pltpu.SemaphoreType.DMA,
        ],
        compiler_params=pltpu.CompilerParams(collective_id=collective_id, has_side_effects=True),
        name="gather_" + axis,
    )(x)


def smooth_kernel(
    x_local, fam_local, group,
    owner_ref, mx_ref, my_ref, u_ref, tops_ref, rel_ref, own_ref, t_ref,
):
    step = pl.program_id(0)
    nx, ny = owner_ref.shape
    rows = x_local + HALO
    x0 = lax.axis_index("gx") * x_local
    first = lax.axis_index("fam") * fam_local + step * group

    @pl.when(step == 0)
    def _():
        own_ref[0:x_local, :] = owner_ref[
            pl.ds(pl.multiple_of(x0, x_local), x_local), :
        ].astype(jnp.float32)
        after = lax.rem(x0 + x_local, nx)
        before = lax.rem(x0 + nx - 16, nx)
        right = owner_ref[pl.ds(pl.multiple_of(after, 16), 16), :].astype(jnp.float32)[0:HALO]
        left = owner_ref[pl.ds(pl.multiple_of(before, 16), 16), :].astype(jnp.float32)[HALO:16]
        place = lax.broadcasted_iota(jnp.int32, (HALO, ny), 0)
        own_ref[x_local:rows, :] = jnp.where(place < HALO // 2, right, left)
        tops_ref[...] = jnp.full(tops_ref.shape, BIG, jnp.float32)

    shift = jnp.full((nx, ny), first.astype(jnp.float32), jnp.float32).astype(jnp.bfloat16)
    rel_ref[...] = owner_ref[...] - shift
    mx = mx_ref[...]
    for j in range(group):
        chi = jnp.where(
            rel_ref[...] == jnp.bfloat16(j), jnp.bfloat16(1), jnp.bfloat16(0)
        )
        both = jnp.dot(mx, chi, preferred_element_type=jnp.float32)
        t_ref[j * rows : (j + 1) * rows, :] = both[:rows] + both[rows:]
    t = t_ref[...].astype(jnp.bfloat16)
    s = jnp.dot(t, my_ref[0], preferred_element_type=jnp.float32)
    for part in range(1, my_ref.shape[0]):
        s = s + jnp.dot(t, my_ref[part], preferred_element_type=jnp.float32)
    t_ref[...] = s
    base = first.astype(jnp.float32)
    for r in range(rows // 8):
        strip = slice(8 * r, 8 * r + 8)
        own = own_ref[strip, :] - base
        high, second = tops_ref[0, strip, :], tops_ref[1, strip, :]
        for j in range(group):
            u = t_ref[j * rows + 8 * r : j * rows + 8 * r + 8, :]
            u = u + jnp.where(own == float(j), fidelity, 0.0)
            u_ref[j, strip, :] = u
            second = jnp.maximum(second, jnp.minimum(high, u))
            high = jnp.maximum(high, u)
        tops_ref[0, strip, :] = high
        tops_ref[1, strip, :] = second


def smoothed(owner, mx, my, x_local, fam_local):
    nx, ny = owner.shape
    rows = x_local + HALO
    group = min(8, fam_local)
    return pl.pallas_call(
        functools.partial(smooth_kernel, x_local, fam_local, group),
        grid=(fam_local // group,),
        out_shape=(
            jax.ShapeDtypeStruct((fam_local, rows, ny), jnp.float32),
            jax.ShapeDtypeStruct((2, rows, ny), jnp.float32),
        ),
        in_specs=[
            pl.BlockSpec((nx, ny), lambda i: (0, 0)),
            pl.BlockSpec(mx.shape, lambda i: (0, 0)),
            pl.BlockSpec(my.shape, lambda i: (0, 0, 0)),
        ],
        out_specs=(
            pl.BlockSpec((group, rows, ny), lambda i: (i, 0, 0)),
            pl.BlockSpec((2, rows, ny), lambda i: (0, 0, 0)),
        ),
        scratch_shapes=[
            pltpu.VMEM((nx, ny), jnp.bfloat16),
            pltpu.VMEM((rows, ny), jnp.float32),
            pltpu.VMEM((group * rows, ny), jnp.float32),
        ],
        compiler_params=pltpu.CompilerParams(vmem_limit_bytes=40 * 2**20),
        name="smooth",
    )(owner, mx, my)


def redistance_kernel(x_local, group, tops_ref, u_ref, out_ref, top_ref, phi_ref, sig_ref, half_ref):
    rows, ny = u_ref.shape[1:]
    chunks = ny // LANES
    strips = rows // 8

    @pl.when(pl.program_id(0) == 0)
    def _():
        for r in range(strips):
            strip = slice(8 * r, 8 * r + 8)
            high, second = tops_ref[0, 0, strip, :], tops_ref[0, 1, strip, :]
            for part in range(1, tops_ref.shape[0]):
                other, third = tops_ref[part, 0, strip, :], tops_ref[part, 1, strip, :]
                second = jnp.maximum(jnp.minimum(high, other), jnp.maximum(second, third))
                high = jnp.maximum(high, other)
            top_ref[0, strip, :] = high
            top_ref[1, strip, :] = second

    lane = lax.broadcasted_iota(jnp.int32, (8, LANES), 1)
    is_first, is_last = lane == 0, lane == LANES - 1

    def put(slot, r, c, value):
        phi_ref[slot, c, 8 * r + HALO : 8 * r + HALO + 8, :] = value
        if r == strips - 1:
            phi_ref[slot, c, 0:HALO, :] = value

    def one(j, carry):
        for r in range(strips):
            for c in range(chunks):
                rs, cs = slice(8 * r, 8 * r + 8), slice(c * LANES, (c + 1) * LANES)
                u = u_ref[j, rs, cs]
                top1 = top_ref[0, rs, cs]
                phi = scale_factor * (u - jnp.where(u >= top1, top_ref[1, rs, cs], top1))
                put(0, r, c, phi)
                sig_ref[c, rs, :] = jnp.where(phi > 0.0, 1.0, -1.0)
                half_ref[c, rs, :] = phi * (step_size * lax.rsqrt(phi * phi + 1.0))
        for sweep in range(SWEEPS):
            src, dst = sweep % 2, (sweep + 1) % 2
            final = sweep == SWEEPS - 1
            for r in range(x_local // 8 if final else strips):
                rs = slice(8 * r, 8 * r + 8)
                mid = [phi_ref[src, c, 8 * r + HALO : 8 * r + HALO + 8, :] for c in range(chunks)]
                to_right = [pltpu.roll(v, 1, 1) for v in mid]
                to_left = [pltpu.roll(v, LANES - 1, 1) for v in mid]
                for c in range(chunks):
                    sig, half, centre = sig_ref[c, rs, :], half_ref[c, rs, :], mid[c]
                    y_low = jnp.where(is_first, to_right[c - 1], to_right[c])
                    y_high = jnp.where(is_last, to_left[(c + 1) % chunks], to_left[c])
                    x_low = phi_ref[src, c, 8 * r + HALO - 1 : 8 * r + HALO + 7, :]
                    if r == strips - 1:
                        x_high = phi_ref[src, c, 1:9, :]
                    else:
                        x_high = phi_ref[src, c, 8 * r + HALO + 1 : 8 * r + HALO + 9, :]
                    here = centre * sig
                    gx = jnp.maximum(here - jnp.minimum(x_low * sig, x_high * sig), 1e-18)
                    gy = jnp.maximum(here - jnp.minimum(y_low * sig, y_high * sig), 1e-18)
                    square = gx * gx + gy * gy
                    grad = square * lax.rsqrt(square)
                    new = centre - half * (grad - 1.0)
                    if final:
                        out_ref[j, rs, c * LANES : (c + 1) * LANES] = new
                    else:
                        put(dst, r, c, new)
        return carry

    lax.fori_loop(0, group, one, 0)


def redistanced(tops, u, x_local):
    fam_local, rows, ny = u.shape
    group = min(8, fam_local)
    chunks = ny // LANES
    return pl.pallas_call(
        functools.partial(redistance_kernel, x_local, group),
        grid=(fam_local // group,),
        out_shape=jax.ShapeDtypeStruct((fam_local, x_local, ny), jnp.float32),
        in_specs=[
            pl.BlockSpec(tops.shape, lambda i: (0, 0, 0, 0)),
            pl.BlockSpec((group, rows, ny), lambda i: (i, 0, 0)),
        ],
        out_specs=pl.BlockSpec((group, x_local, ny), lambda i: (i, 0, 0)),
        scratch_shapes=[
            pltpu.VMEM((2, rows, ny), jnp.float32),
            pltpu.VMEM((2, chunks, rows + HALO, LANES), jnp.float32),
            pltpu.VMEM((chunks, rows, LANES), jnp.float32),
            pltpu.VMEM((chunks, rows, LANES), jnp.float32),
        ],
        compiler_params=pltpu.CompilerParams(vmem_limit_bytes=40 * 2**20),
        name="redistance",
    )(tops, u)


def body(labels, family_of_grain, mx, my):
    parts, fams = lax.axis_size("gx"), lax.axis_size("fam")
    nz, x_local, ny = labels.shape
    assert nz == 1
    nx = x_local * parts
    fam_local = F // fams
    owner = owners(labels[0], family_of_grain.reshape(-1, LANES))
    owner = gathered(owner, "gx", parts, 0).reshape(nx, ny)
    u, tops = smoothed(owner, mx[0], my, x_local, fam_local)
    tops = gathered(tops, "fam", fams, 1)
    return redistanced(tops, u, x_local)[:, None]


def solution(mesh):
    def run(labels, family_of_grain):
        nz, nx, ny = labels.shape
        parts = mesh.shape["gx"]
        high, low = smoothing(nx)
        rows = ring_rows(nx // parts, nx, parts)
        mx = jnp.asarray(np.concatenate([high[rows], low[rows]], axis=1))
        my = jnp.asarray(smoothing(ny)[0][None])
        mapped = jax.shard_map(
            body,
            mesh=mesh,
            in_specs=(P(None, "gx", None), P(), P("gx", None, None), P()),
            out_specs=P("fam", None, "gx", None),
            check_vma=False,
        )
        return mapped(labels, family_of_grain, mx, my)

    return run
```

```python
import functools

import jax
import jax.numpy as jnp
import ml_dtypes
import numpy as np
from jax import lax
from jax.experimental import pallas as pl
from jax.experimental.pallas import tpu as pltpu
from jax.sharding import PartitionSpec as P

F = 256
WIDTH = 2
SWEEPS = 3
HALO = 8
LANES = 128
BIG = -1e30
VMEM = 60 * 2**20
MESH = pl.DeviceIdType.MESH

fidelity = 0.25
scale_factor = 8.0
step_size = 0.5


def smoothing(count):
    idx = np.arange(count).astype(np.float32)
    angle = (np.float32(2.0 * np.pi) * np.outer(idx, idx)) / np.float32(count)
    cas = (np.cos(angle) + np.sin(angle)).astype(ml_dtypes.bfloat16).astype(np.float64)
    freq = np.arange(count)
    mirror = np.minimum(freq, count - freq).astype(np.float64)
    sigma = WIDTH / 2.0
    gauss = np.exp(-2.0 * np.pi**2 * sigma**2 * mirror**2 / (count * count))
    full = (cas * gauss) @ cas.T / count
    high = full.astype(ml_dtypes.bfloat16)
    low = (full - high.astype(np.float64)).astype(ml_dtypes.bfloat16)
    return high, low


def ring_rows(x_local, count, parts):
    rows = x_local + HALO
    out = []
    for part in range(parts):
        r = np.arange(rows)
        x = part * x_local + np.where(r < x_local + HALO // 2, r, r - rows)
        out.append(x % count)
    return np.stack(out)


def owner_kernel(labels_ref, table_ref, out_ref):
    rows, cols = labels_ref.shape
    words = []
    for k in range(table_ref.shape[0] // 4):
        quad = [table_ref[4 * k + b : 4 * k + b + 1, :] for b in range(4)]
        word = quad[0] + quad[1] * 2**8 + quad[2] * 2**16 + lax.shift_left(quad[3], 24)
        words.append(jnp.broadcast_to(word, (rows, LANES)))
    for c in range(cols // LANES):
        lab = labels_ref[:, c * LANES : (c + 1) * LANES]
        lane = lax.bitwise_and(lab, LANES - 1)
        page = lax.shift_right_logical(lab, LANES.bit_length() - 1)
        which = lax.shift_right_logical(page, 2)
        place = lax.bitwise_and(page, 3) * 8
        acc = jnp.take_along_axis(words[0], lane, axis=1)
        for k in range(1, len(words)):
            acc = jnp.where(which == k, jnp.take_along_axis(words[k], lane, axis=1), acc)
        acc = lax.bitwise_and(lax.shift_right_logical(acc, place), 255)
        out_ref[:, c * LANES : (c + 1) * LANES] = acc.astype(jnp.float32).astype(out_ref.dtype)


def owners(labels, table):
    return pl.pallas_call(
        owner_kernel,
        out_shape=jax.ShapeDtypeStruct(labels.shape, jnp.bfloat16),
        compiler_params=pltpu.CompilerParams(vmem_limit_bytes=VMEM),
        name="owner_lookup",
    )(labels, table)


def gather_kernel(axis, size, x_ref, out_ref, send_sem, recv_sem, local_sem):
    me = lax.axis_index(axis)
    chips = size // 2
    chip, core = me // 2, lax.rem(me, 2)
    beside = 2 * chip + 1 - core
    others = [2 * lax.rem(chip + d, chips) + core for d in range(1, chips)]
    barrier = pltpu.get_barrier_semaphore()
    for device in [beside, *others]:
        pl.semaphore_signal(barrier, inc=1, device_id={axis: device}, device_id_type=MESH)
    local = pltpu.make_async_copy(x_ref, out_ref.at[me], local_sem)
    local.start()
    pl.semaphore_wait(barrier, chips)

    def send(src, slab, device, k):
        copy = pltpu.make_async_remote_copy(
            src_ref=src,
            dst_ref=out_ref.at[slab],
            send_sem=send_sem.at[k],
            recv_sem=recv_sem.at[k],
            device_id={axis: device},
            device_id_type=MESH,
        )
        copy.start()
        return copy

    far = [send(x_ref, me, device, d) for d, device in enumerate(others)]
    near = [send(x_ref, me, beside, chips - 1)]
    for d in range(1, chips):
        far[d - 1].wait_recv()
        slab = 2 * lax.rem(chip + chips - d, chips) + core
        near.append(send(out_ref.at[slab], slab, beside, chips - 1 + d))
    local.wait()
    for copy in far:
        copy.wait_send()
    for copy in near:
        copy.wait()


def gathered(x, axis, size, collective_id):
    return pl.pallas_call(
        functools.partial(gather_kernel, axis, size),
        out_shape=jax.ShapeDtypeStruct((size, *x.shape), x.dtype),
        in_specs=[pl.BlockSpec(memory_space=pltpu.VMEM)],
        out_specs=pl.BlockSpec(memory_space=pltpu.VMEM),
        scratch_shapes=[
            pltpu.SemaphoreType.DMA((size - 1,)),
            pltpu.SemaphoreType.DMA((size - 1,)),
            pltpu.SemaphoreType.DMA,
        ],
        compiler_params=pltpu.CompilerParams(
            collective_id=collective_id, has_side_effects=True, vmem_limit_bytes=VMEM
        ),
        name="gather_" + axis,
    )(x)


def merge_kernel(axis, size, x_ref, out_ref, recv_ref, send_sem, recv_sem, back_send, back_recv):
    me = lax.axis_index(axis)
    others = [lax.rem(me + k, size) for k in range(1, size)]
    barrier = pltpu.get_barrier_semaphore()
    for device in others:
        pl.semaphore_signal(barrier, inc=1, device_id={axis: device}, device_id_type=MESH)
    pl.semaphore_wait(barrier, size - 1)

    def send(src, dst, sems, k, device):
        copy = pltpu.make_async_remote_copy(
            src_ref=src,
            dst_ref=dst,
            send_sem=sems[0].at[k],
            recv_sem=sems[1].at[k],
            device_id={axis: device},
            device_id_type=MESH,
        )
        copy.start()
        return copy

    there = [
        send(x_ref.at[device], recv_ref.at[k], (send_sem, recv_sem), k, device)
        for k, device in enumerate(others)
    ]
    high, second = x_ref[me, 0], x_ref[me, 1]
    for k in range(size - 1):
        there[k].wait_recv()
        other, third = recv_ref[k, 0], recv_ref[k, 1]
        second = jnp.maximum(jnp.minimum(high, other), jnp.maximum(second, third))
        high = jnp.maximum(high, other)
    out_ref[me, 0] = high
    out_ref[me, 1] = second
    back = [
        send(out_ref.at[me], out_ref.at[me], (back_send, back_recv), k, device)
        for k, device in enumerate(others)
    ]
    for copy in there:
        copy.wait_send()
    for copy in back:
        copy.wait()


def merged(x, axis, size, collective_id):
    return pl.pallas_call(
        functools.partial(merge_kernel, axis, size),
        out_shape=jax.ShapeDtypeStruct(x.shape, x.dtype),
        in_specs=[pl.BlockSpec(memory_space=pltpu.VMEM)],
        out_specs=pl.BlockSpec(memory_space=pltpu.VMEM),
        scratch_shapes=[pltpu.VMEM((size - 1, *x.shape[1:]), x.dtype)]
        + [pltpu.SemaphoreType.DMA((size - 1,))] * 4,
        compiler_params=pltpu.CompilerParams(
            collective_id=collective_id, has_side_effects=True, vmem_limit_bytes=VMEM
        ),
        name="merge_" + axis,
    )(x)


def tile_place(k, per_piece):
    row = 8 * (k % per_piece)
    return k // per_piece, slice(row, row + 8)


def smooth_kernel(
    x_local, fam_local, group,
    owner_ref, mx_ref, my_ref, u_ref, tops_ref, rel_ref, own_ref, t_ref,
):
    step = pl.program_id(0)
    nx, ny = owner_ref.shape
    rows = x_local + HALO
    x0 = lax.axis_index("gx") * x_local
    first = lax.axis_index("fam") * fam_local + step * group

    @pl.when(step == 0)
    def _():
        own_ref[0:x_local, :] = owner_ref[
            pl.ds(pl.multiple_of(x0, x_local), x_local), :
        ].astype(jnp.float32)
        after = lax.rem(x0 + x_local, nx)
        before = lax.rem(x0 + nx - 16, nx)
        right = owner_ref[pl.ds(pl.multiple_of(after, 16), 16), :].astype(jnp.float32)[0:HALO]
        left = owner_ref[pl.ds(pl.multiple_of(before, 16), 16), :].astype(jnp.float32)[HALO:16]
        place = lax.broadcasted_iota(jnp.int32, (HALO, ny), 0)
        own_ref[x_local:rows, :] = jnp.where(place < HALO // 2, right, left)
        tops_ref[...] = jnp.full(tops_ref.shape, BIG, jnp.float32)

    shift = jnp.full((nx, ny), first.astype(jnp.float32), jnp.float32).astype(jnp.bfloat16)
    rel_ref[...] = owner_ref[...] - shift
    mx = mx_ref[0]
    for j in range(group):
        chi = jnp.where(
            rel_ref[...] == jnp.bfloat16(j), jnp.bfloat16(1), jnp.bfloat16(0)
        )
        both = jnp.dot(mx, chi, preferred_element_type=jnp.float32)
        t_ref[j * rows : (j + 1) * rows, :] = both[:rows] + both[rows:]
    t = t_ref[...].astype(jnp.bfloat16)
    s = jnp.dot(t, my_ref[0], preferred_element_type=jnp.float32)
    for part in range(1, my_ref.shape[0]):
        s = s + jnp.dot(t, my_ref[part], preferred_element_type=jnp.float32)
    t_ref[...] = s
    base = first.astype(jnp.float32)
    per_piece = tops_ref.shape[2] // 8
    for r in range(rows // 8):
        strip = slice(8 * r, 8 * r + 8)
        for c in range(ny // LANES):
            cols = slice(c * LANES, (c + 1) * LANES)
            piece, place = tile_place(r * (ny // LANES) + c, per_piece)
            own = own_ref[strip, cols] - base
            high, second = tops_ref[piece, 0, place, :], tops_ref[piece, 1, place, :]
            for j in range(group):
                u = t_ref[j * rows + 8 * r : j * rows + 8 * r + 8, cols]
                u = u + jnp.where(own == float(j), fidelity, 0.0)
                u_ref[j, strip, cols] = u
                second = jnp.maximum(second, jnp.minimum(high, u))
                high = jnp.maximum(high, u)
            tops_ref[piece, 0, place, :] = high
            tops_ref[piece, 1, place, :] = second


def smoothed(owner, mx, my, x_local, fam_local, fams):
    nx, ny = owner.shape
    rows = x_local + HALO
    group = min(8, fam_local)
    tiles = rows * ny // (8 * LANES)
    pieces = (fams, 2, 8 * (-(-tiles // fams)), LANES)
    return pl.pallas_call(
        functools.partial(smooth_kernel, x_local, fam_local, group),
        grid=(fam_local // group,),
        out_shape=(
            jax.ShapeDtypeStruct((fam_local, rows, ny), jnp.float32),
            jax.ShapeDtypeStruct(pieces, jnp.float32),
        ),
        in_specs=[
            pl.BlockSpec((nx, ny), lambda i: (0, 0)),
            pl.BlockSpec((1, *mx.shape[1:]), lambda i: (lax.axis_index("gx"), 0, 0)),
            pl.BlockSpec(my.shape, lambda i: (0, 0, 0)),
        ],
        out_specs=(
            pl.BlockSpec((group, rows, ny), lambda i: (i, 0, 0)),
            pl.BlockSpec(pieces, lambda i: (0, 0, 0, 0)),
        ),
        scratch_shapes=[
            pltpu.VMEM((nx, ny), jnp.bfloat16),
            pltpu.VMEM((rows, ny), jnp.float32),
            pltpu.VMEM((group * rows, ny), jnp.float32),
        ],
        compiler_params=pltpu.CompilerParams(vmem_limit_bytes=VMEM),
        name="smooth",
    )(owner, mx, my)


def redistance_kernel(x_local, group, tops_ref, u_ref, out_ref, phi_ref, sig_ref, half_ref):
    rows, ny = u_ref.shape[1:]
    chunks = ny // LANES
    strips = rows // 8

    per_piece = tops_ref.shape[2] // 8
    lane = lax.broadcasted_iota(jnp.int32, (8, LANES), 1)
    is_first, is_last = lane == 0, lane == LANES - 1

    def put(slot, r, c, value):
        phi_ref[slot, c, 8 * r + HALO : 8 * r + HALO + 8, :] = value
        if r == strips - 1:
            phi_ref[slot, c, 0:HALO, :] = value

    def one(j, carry):
        for r in range(strips):
            for c in range(chunks):
                rs, cs = slice(8 * r, 8 * r + 8), slice(c * LANES, (c + 1) * LANES)
                u = u_ref[j, rs, cs]
                piece, place = tile_place(r * chunks + c, per_piece)
                top1, top2 = tops_ref[piece, 0, place, :], tops_ref[piece, 1, place, :]
                phi = scale_factor * (u - jnp.where(u >= top1, top2, top1))
                put(0, r, c, phi)
                sig_ref[c, rs, :] = jnp.where(phi > 0.0, 1.0, -1.0)
                half_ref[c, rs, :] = phi * (step_size * lax.rsqrt(phi * phi + 1.0))
        for sweep in range(SWEEPS):
            src, dst = sweep % 2, (sweep + 1) % 2
            final = sweep == SWEEPS - 1
            for r in range(x_local // 8 if final else strips):
                rs = slice(8 * r, 8 * r + 8)
                mid = [phi_ref[src, c, 8 * r + HALO : 8 * r + HALO + 8, :] for c in range(chunks)]
                to_right = [pltpu.roll(v, 1, 1) for v in mid]
                to_left = [pltpu.roll(v, LANES - 1, 1) for v in mid]
                for c in range(chunks):
                    sig, half, centre = sig_ref[c, rs, :], half_ref[c, rs, :], mid[c]
                    y_low = jnp.where(is_first, to_right[c - 1], to_right[c])
                    y_high = jnp.where(is_last, to_left[(c + 1) % chunks], to_left[c])
                    x_low = phi_ref[src, c, 8 * r + HALO - 1 : 8 * r + HALO + 7, :]
                    if r == strips - 1:
                        x_high = phi_ref[src, c, 1:9, :]
                    else:
                        x_high = phi_ref[src, c, 8 * r + HALO + 1 : 8 * r + HALO + 9, :]
                    here = centre * sig
                    gx = jnp.maximum(here - jnp.minimum(x_low * sig, x_high * sig), 1e-18)
                    gy = jnp.maximum(here - jnp.minimum(y_low * sig, y_high * sig), 1e-18)
                    square = gx * gx + gy * gy
                    grad = square * lax.rsqrt(square)
                    new = centre - half * (grad - 1.0)
                    if final:
                        out_ref[j, rs, c * LANES : (c + 1) * LANES] = new
                    else:
                        put(dst, r, c, new)
        return carry

    lax.fori_loop(0, group, one, 0)


def redistanced(tops, u, x_local):
    fam_local, rows, ny = u.shape
    group = min(8, fam_local)
    chunks = ny // LANES
    return pl.pallas_call(
        functools.partial(redistance_kernel, x_local, group),
        grid=(fam_local // group,),
        out_shape=jax.ShapeDtypeStruct((fam_local, x_local, ny), jnp.float32),
        in_specs=[
            pl.BlockSpec(tops.shape, lambda i: (0, 0, 0, 0)),
            pl.BlockSpec((group, rows, ny), lambda i: (i, 0, 0)),
        ],
        out_specs=pl.BlockSpec((group, x_local, ny), lambda i: (i, 0, 0)),
        scratch_shapes=[
            pltpu.VMEM((2, chunks, rows + HALO, LANES), jnp.float32),
            pltpu.VMEM((chunks, rows, LANES), jnp.float32),
            pltpu.VMEM((chunks, rows, LANES), jnp.float32),
        ],
        compiler_params=pltpu.CompilerParams(vmem_limit_bytes=VMEM),
        name="redistance",
    )(tops, u)


def body(labels, family_of_grain, mx, my):
    parts, fams = lax.axis_size("gx"), lax.axis_size("fam")
    nz, x_local, ny = labels.shape
    assert nz == 1
    nx = x_local * parts
    fam_local = F // fams
    owner = owners(labels[0], family_of_grain.reshape(-1, LANES))
    owner = gathered(owner, "gx", parts, 0).reshape(nx, ny)
    u, tops = smoothed(owner, mx, my, x_local, fam_local, fams)
    tops = merged(tops, "fam", fams, 1)
    return redistanced(tops, u, x_local)[:, None]


def solution(mesh):
    def run(labels, family_of_grain):
        nz, nx, ny = labels.shape
        parts = mesh.shape["gx"]
        high, low = smoothing(nx)
        rows = ring_rows(nx // parts, nx, parts)
        mx = jnp.asarray(np.concatenate([high[rows], low[rows]], axis=1))
        my = jnp.asarray(smoothing(ny)[0][None])
        mapped = jax.shard_map(
            body,
            mesh=mesh,
            in_specs=(P(None, "gx", None), P(), P(), P()),
            out_specs=P("fam", None, "gx", None),
            check_vma=False,
        )
        return mapped(labels, family_of_grain, mx, my)

    return run
```

```python
import functools

import jax
import jax.numpy as jnp
import ml_dtypes
import numpy as np
from jax import lax
from jax.experimental import pallas as pl
from jax.experimental.pallas import tpu as pltpu
from jax.sharding import PartitionSpec as P

F = 256
WIDTH = 2
SWEEPS = 3
HALO = 8
LANES = 128
BIG = -1e30
VMEM = 60 * 2**20
MESH = pl.DeviceIdType.MESH

fidelity = 0.25
scale_factor = 8.0
step_size = 0.5


def smoothing(count):
    idx = np.arange(count).astype(np.float32)
    angle = (np.float32(2.0 * np.pi) * np.outer(idx, idx)) / np.float32(count)
    cas = (np.cos(angle) + np.sin(angle)).astype(ml_dtypes.bfloat16).astype(np.float64)
    freq = np.arange(count)
    mirror = np.minimum(freq, count - freq).astype(np.float64)
    sigma = WIDTH / 2.0
    gauss = np.exp(-2.0 * np.pi**2 * sigma**2 * mirror**2 / (count * count))
    full = (cas * gauss) @ cas.T / count
    high = full.astype(ml_dtypes.bfloat16)
    low = (full - high.astype(np.float64)).astype(ml_dtypes.bfloat16)
    return high, low


def ring_rows(x_local, count, parts):
    rows = x_local + HALO
    r = np.arange(rows).reshape(8, rows // 8).T.reshape(-1)
    away = np.where(r < x_local + HALO // 2, r, r - rows)
    return np.stack([(part * x_local + away) % count for part in range(parts)])


def look_up(labels_ref, table_ref, out_ref):
    rows, cols = labels_ref.shape
    words = []
    for k in range(table_ref.shape[0] // 4):
        quad = [table_ref[4 * k + b : 4 * k + b + 1, :] for b in range(4)]
        word = quad[0] + quad[1] * 2**8 + quad[2] * 2**16 + lax.shift_left(quad[3], 24)
        words.append(jnp.broadcast_to(word, (rows, LANES)))
    for c in range(cols // LANES):
        lab = labels_ref[:, c * LANES : (c + 1) * LANES]
        lane = lax.bitwise_and(lab, LANES - 1)
        page = lax.shift_right_logical(lab, LANES.bit_length() - 1)
        which = lax.shift_right_logical(page, 2)
        place = lax.bitwise_and(page, 3) * 8
        acc = jnp.take_along_axis(words[0], lane, axis=1)
        for k in range(1, len(words)):
            acc = jnp.where(which == k, jnp.take_along_axis(words[k], lane, axis=1), acc)
        acc = lax.bitwise_and(lax.shift_right_logical(acc, place), 255)
        out_ref[:, c * LANES : (c + 1) * LANES] = acc.astype(jnp.float32).astype(out_ref.dtype)


def gather_kernel(axis, size, labels_ref, table_ref, out_ref, x_ref, send_sem, recv_sem, local_sem):
    me = lax.axis_index(axis)
    chips = size // 2
    chip, core = me // 2, lax.rem(me, 2)
    beside = 2 * chip + 1 - core
    others = [2 * lax.rem(chip + d, chips) + core for d in range(1, chips)]
    barrier = pltpu.get_barrier_semaphore()
    for device in [beside, *others]:
        pl.semaphore_signal(barrier, inc=1, device_id={axis: device}, device_id_type=MESH)
    look_up(labels_ref, table_ref, x_ref)
    local = pltpu.make_async_copy(x_ref, out_ref.at[me], local_sem)
    local.start()
    pl.semaphore_wait(barrier, chips)

    def send(src, slab, device, k):
        copy = pltpu.make_async_remote_copy(
            src_ref=src,
            dst_ref=out_ref.at[slab],
            send_sem=send_sem.at[k],
            recv_sem=recv_sem.at[k],
            device_id={axis: device},
            device_id_type=MESH,
        )
        copy.start()
        return copy

    far = [send(x_ref, me, device, d) for d, device in enumerate(others)]
    near = [send(x_ref, me, beside, chips - 1)]
    for d in range(1, chips):
        far[d - 1].wait_recv()
        slab = 2 * lax.rem(chip + chips - d, chips) + core
        near.append(send(out_ref.at[slab], slab, beside, chips - 1 + d))
    local.wait()
    for copy in far:
        copy.wait_send()
    for copy in near:
        copy.wait()


def gathered_owners(labels, table, axis, size, collective_id):
    return pl.pallas_call(
        functools.partial(gather_kernel, axis, size),
        out_shape=jax.ShapeDtypeStruct((size, *labels.shape), jnp.bfloat16),
        in_specs=[pl.BlockSpec(memory_space=pltpu.VMEM)] * 2,
        out_specs=pl.BlockSpec(memory_space=pltpu.VMEM),
        scratch_shapes=[
            pltpu.VMEM(labels.shape, jnp.bfloat16),
            pltpu.SemaphoreType.DMA((size - 1,)),
            pltpu.SemaphoreType.DMA((size - 1,)),
            pltpu.SemaphoreType.DMA,
        ],
        compiler_params=pltpu.CompilerParams(
            collective_id=collective_id, has_side_effects=True, vmem_limit_bytes=VMEM
        ),
        name="gather_" + axis,
    )(labels, table)


def merge_kernel(axis, size, x_ref, out_ref, recv_ref, send_sem, recv_sem, back_send, back_recv):
    me = lax.axis_index(axis)
    others = [lax.rem(me + k, size) for k in range(1, size)]
    barrier = pltpu.get_barrier_semaphore()
    for device in others:
        pl.semaphore_signal(barrier, inc=1, device_id={axis: device}, device_id_type=MESH)
    pl.semaphore_wait(barrier, size - 1)

    def send(src, dst, sems, k, device):
        copy = pltpu.make_async_remote_copy(
            src_ref=src,
            dst_ref=dst,
            send_sem=sems[0].at[k],
            recv_sem=sems[1].at[k],
            device_id={axis: device},
            device_id_type=MESH,
        )
        copy.start()
        return copy

    there = [
        send(x_ref.at[device], recv_ref.at[k], (send_sem, recv_sem), k, device)
        for k, device in enumerate(others)
    ]
    high, second = x_ref[me, 0], x_ref[me, 1]
    for k in range(size - 1):
        there[k].wait_recv()
        other, third = recv_ref[k, 0], recv_ref[k, 1]
        second = jnp.maximum(jnp.minimum(high, other), jnp.maximum(second, third))
        high = jnp.maximum(high, other)
    out_ref[me, 0] = high
    out_ref[me, 1] = second
    back = [
        send(out_ref.at[me], out_ref.at[me], (back_send, back_recv), k, device)
        for k, device in enumerate(others)
    ]
    for copy in there:
        copy.wait_send()
    for copy in back:
        copy.wait()


def merged(x, axis, size, collective_id):
    return pl.pallas_call(
        functools.partial(merge_kernel, axis, size),
        out_shape=jax.ShapeDtypeStruct(x.shape, x.dtype),
        in_specs=[pl.BlockSpec(memory_space=pltpu.VMEM)],
        out_specs=pl.BlockSpec(memory_space=pltpu.VMEM),
        scratch_shapes=[pltpu.VMEM((size - 1, *x.shape[1:]), x.dtype)]
        + [pltpu.SemaphoreType.DMA((size - 1,))] * 4,
        compiler_params=pltpu.CompilerParams(
            collective_id=collective_id, has_side_effects=True, vmem_limit_bytes=VMEM
        ),
        name="merge_" + axis,
    )(x)


def tile_place(k, per_piece):
    row = 8 * (k % per_piece)
    return k // per_piece, slice(row, row + 8)


def smooth_kernel(
    x_local, fam_local, group,
    owner_ref, mx_ref, my_ref, u_ref, tops_ref, rel_ref, own_ref, ring_ref, t_ref,
):
    step = pl.program_id(0)
    nx, ny = owner_ref.shape
    rows = x_local + HALO
    x0 = lax.axis_index("gx") * x_local
    first = lax.axis_index("fam") * fam_local + step * group

    @pl.when(step == 0)
    def _():
        mine = owner_ref[pl.ds(pl.multiple_of(x0, x_local), x_local), :].astype(jnp.float32)
        after = lax.rem(x0 + x_local, nx)
        before = lax.rem(x0 + nx - 16, nx)
        right = owner_ref[pl.ds(pl.multiple_of(after, 16), 16), :].astype(jnp.float32)[0:HALO]
        left = owner_ref[pl.ds(pl.multiple_of(before, 16), 16), :].astype(jnp.float32)[HALO:16]
        place = lax.broadcasted_iota(jnp.int32, (HALO, ny), 0)
        halo = jnp.where(place < HALO // 2, right, left)
        strips = rows // 8
        for c in range(ny // LANES):
            cols = slice(c * LANES, (c + 1) * LANES)
            ring_ref[c, 0:x_local, :] = mine[:, cols]
            ring_ref[c, x_local:rows, :] = halo[:, cols]
            for r in range(strips):
                own_ref[8 * r : 8 * r + 8, cols] = ring_ref[c, pl.ds(r, 8, stride=strips), :]
        tops_ref[...] = jnp.full(tops_ref.shape, BIG, jnp.float32)

    shift = jnp.full((nx, ny), first.astype(jnp.float32), jnp.float32).astype(jnp.bfloat16)
    rel_ref[...] = owner_ref[...] - shift
    mx = mx_ref[0]
    for j in range(group):
        chi = jnp.where(
            rel_ref[...] == jnp.bfloat16(j), jnp.bfloat16(1), jnp.bfloat16(0)
        )
        both = jnp.dot(mx, chi, preferred_element_type=jnp.float32)
        t_ref[j * rows : (j + 1) * rows, :] = both[:rows] + both[rows:]
    t = t_ref[...].astype(jnp.bfloat16)
    s = jnp.dot(t, my_ref[0], preferred_element_type=jnp.float32)
    for part in range(1, my_ref.shape[0]):
        s = s + jnp.dot(t, my_ref[part], preferred_element_type=jnp.float32)
    t_ref[...] = s
    base = first.astype(jnp.float32)
    per_piece = tops_ref.shape[2] // 8
    for r in range(rows // 8):
        strip = slice(8 * r, 8 * r + 8)
        for c in range(ny // LANES):
            cols = slice(c * LANES, (c + 1) * LANES)
            piece, place = tile_place(r * (ny // LANES) + c, per_piece)
            own = own_ref[strip, cols] - base
            high, second = tops_ref[piece, 0, place, :], tops_ref[piece, 1, place, :]
            for j in range(group):
                u = t_ref[j * rows + 8 * r : j * rows + 8 * r + 8, cols]
                u = u + jnp.where(own == float(j), fidelity, 0.0)
                u_ref[j, strip, cols] = u
                second = jnp.maximum(second, jnp.minimum(high, u))
                high = jnp.maximum(high, u)
            tops_ref[piece, 0, place, :] = high
            tops_ref[piece, 1, place, :] = second


def smoothed(owner, mx, my, x_local, fam_local, fams):
    nx, ny = owner.shape
    rows = x_local + HALO
    group = min(8, fam_local)
    tiles = rows * ny // (8 * LANES)
    pieces = (fams, 2, 8 * (-(-tiles // fams)), LANES)
    return pl.pallas_call(
        functools.partial(smooth_kernel, x_local, fam_local, group),
        grid=(fam_local // group,),
        out_shape=(
            jax.ShapeDtypeStruct((fam_local, rows, ny), jnp.float32),
            jax.ShapeDtypeStruct(pieces, jnp.float32),
        ),
        in_specs=[
            pl.BlockSpec((nx, ny), lambda i: (0, 0)),
            pl.BlockSpec((1, *mx.shape[1:]), lambda i: (lax.axis_index("gx"), 0, 0)),
            pl.BlockSpec(my.shape, lambda i: (0, 0, 0)),
        ],
        out_specs=(
            pl.BlockSpec((group, rows, ny), lambda i: (i, 0, 0)),
            pl.BlockSpec(pieces, lambda i: (0, 0, 0, 0)),
        ),
        scratch_shapes=[
            pltpu.VMEM((nx, ny), jnp.bfloat16),
            pltpu.VMEM((rows, ny), jnp.float32),
            pltpu.VMEM((ny // LANES, rows, LANES), jnp.float32),
            pltpu.VMEM((group * rows, ny), jnp.float32),
        ],
        compiler_params=pltpu.CompilerParams(vmem_limit_bytes=VMEM),
        name="smooth",
    )(owner, mx, my)


def redistance_kernel(
    x_local, group, tops_ref, u_ref, out_ref, first_ref, half_ref, phi_ref, order_ref, flag_ref
):
    rows, ny = u_ref.shape[1:]
    chunks = ny // LANES
    strips = rows // 8
    per_piece = tops_ref.shape[2] // 8

    def strip(r):
        return slice(8 * r, 8 * r + 8)

    def chunk(c):
        return slice(c * LANES, (c + 1) * LANES)

    peaks = [jnp.full((8, LANES), BIG, jnp.float32) for _ in range(group)]
    for r in range(strips):
        for c in range(chunks):
            piece, place = tile_place(r * chunks + c, per_piece)
            top1, top2 = tops_ref[piece, 0, place, :], tops_ref[piece, 1, place, :]
            for j in range(group):
                u = u_ref[j, strip(r), chunk(c)]
                phi = scale_factor * (u - jnp.where(u >= top1, top2, top1))
                first_ref[j, strip(r), chunk(c)] = phi
                half_ref[j, strip(r), chunk(c)] = phi * (step_size * lax.rsqrt(phi * phi + 1.0))
                peaks[j] = jnp.maximum(peaks[j], phi)
    for j in range(group):
        flag_ref[j] = (jnp.max(peaks[j]) > 0.0).astype(jnp.int32)

    lane = lax.broadcasted_iota(jnp.int32, (8, LANES), 1)
    is_first, is_last = lane == 0, lane == LANES - 1

    def sweeps(j, some_positive):
        for sweep in range(SWEEPS):
            if sweep == 0:
                src = first_ref.at[j]
            else:
                src = phi_ref.at[(sweep + 1) % 2]
            dst = phi_ref.at[sweep % 2]

            def load(r):
                return [src[strip(r), chunk(c)] for c in range(chunks)]

            bottom = [pltpu.roll(v, 1, 0) for v in load(strips - 1)]
            top = [pltpu.roll(v, 7, 0) for v in load(0)]
            low, mid = bottom, load(0)
            for r in range(strips):
                high = top if r == strips - 1 else load(r + 1)
                to_right = [pltpu.roll(v, 1, 1) for v in mid]
                to_left = [pltpu.roll(v, LANES - 1, 1) for v in mid]
                for c in range(chunks):
                    half, here = half_ref[j, strip(r), chunk(c)], mid[c]
                    y_low = jnp.where(is_first, to_right[c - 1], to_right[c])
                    y_high = jnp.where(is_last, to_left[(c + 1) % chunks], to_left[c])
                    if some_positive:
                        sig = jnp.where(half > 0.0, 1.0, -1.0)
                        size = here * sig
                        gx = size - jnp.minimum(low[c] * sig, high[c] * sig)
                        gy = size - jnp.minimum(y_low * sig, y_high * sig)
                    else:
                        gx = jnp.maximum(low[c], high[c]) - here
                        gy = jnp.maximum(y_low, y_high) - here
                    gx, gy = jnp.maximum(gx, 1e-18), jnp.maximum(gy, 1e-18)
                    square = gx * gx + gy * gy
                    grad = square * lax.rsqrt(square)
                    new = here - half * (grad - 1.0)
                    if sweep == SWEEPS - 1:
                        order_ref[c, pl.ds(r, 8, stride=strips), :] = new
                    else:
                        dst[strip(r), chunk(c)] = new
                low, mid = mid, high
        for r in range(x_local // 8):
            for c in range(chunks):
                out_ref[j, strip(r), chunk(c)] = order_ref[c, strip(r), :]

    def one(j, carry):
        @pl.when(flag_ref[j] == 0)
        def _():
            sweeps(j, False)

        @pl.when(flag_ref[j] != 0)
        def _():
            sweeps(j, True)

        return carry

    lax.fori_loop(0, group, one, 0)


def redistanced(tops, u, x_local):
    fam_local, rows, ny = u.shape
    group = min(8, fam_local)
    chunks = ny // LANES
    return pl.pallas_call(
        functools.partial(redistance_kernel, x_local, group),
        grid=(fam_local // group,),
        out_shape=jax.ShapeDtypeStruct((fam_local, x_local, ny), jnp.float32),
        in_specs=[
            pl.BlockSpec(tops.shape, lambda i: (0, 0, 0, 0)),
            pl.BlockSpec((group, rows, ny), lambda i: (i, 0, 0)),
        ],
        out_specs=pl.BlockSpec((group, x_local, ny), lambda i: (i, 0, 0)),
        scratch_shapes=[
            pltpu.VMEM((group, rows, ny), jnp.float32),
            pltpu.VMEM((group, rows, ny), jnp.float32),
            pltpu.VMEM((2, rows, ny), jnp.float32),
            pltpu.VMEM((chunks, rows, LANES), jnp.float32),
            pltpu.SMEM((group,), jnp.int32),
        ],
        compiler_params=pltpu.CompilerParams(vmem_limit_bytes=VMEM),
        name="redistance",
    )(tops, u)


def body(labels, family_of_grain, mx, my):
    parts, fams = lax.axis_size("gx"), lax.axis_size("fam")
    nz, x_local, ny = labels.shape
    assert nz == 1
    nx = x_local * parts
    fam_local = F // fams
    table = family_of_grain.reshape(-1, LANES)
    owner = gathered_owners(labels[0], table, "gx", parts, 0).reshape(nx, ny)
    u, tops = smoothed(owner, mx, my, x_local, fam_local, fams)
    tops = merged(tops, "fam", fams, 1)
    return redistanced(tops, u, x_local)[:, None]


def solution(mesh):
    def run(labels, family_of_grain):
        nz, nx, ny = labels.shape
        parts = mesh.shape["gx"]
        high, low = smoothing(nx)
        rows = ring_rows(nx // parts, nx, parts)
        mx = jnp.asarray(np.concatenate([high[rows], low[rows]], axis=1))
        my = jnp.asarray(smoothing(ny)[0][None])
        mapped = jax.shard_map(
            body,
            mesh=mesh,
            in_specs=(P(None, "gx", None), P(), P(), P()),
            out_specs=P("fam", None, "gx", None),
            check_vma=False,
        )
        return mapped(labels, family_of_grain, mx, my)

    return run
```

```python
import functools

import jax
import jax.numpy as jnp
import ml_dtypes
import numpy as np
from jax import lax
from jax.experimental import pallas as pl
from jax.experimental.pallas import tpu as pltpu
from jax.sharding import PartitionSpec as P

F = 256
WIDTH = 2
SWEEPS = 3
HALO = 8
LANES = 128
BIG = -1e30
VMEM = 60 * 2**20
MESH = pl.DeviceIdType.MESH

fidelity = 0.25
scale_factor = 8.0
step_size = 0.5


def smoothing(count):
    idx = np.arange(count).astype(np.float32)
    angle = (np.float32(2.0 * np.pi) * np.outer(idx, idx)) / np.float32(count)
    cas = (np.cos(angle) + np.sin(angle)).astype(ml_dtypes.bfloat16).astype(np.float64)
    freq = np.arange(count)
    mirror = np.minimum(freq, count - freq).astype(np.float64)
    sigma = WIDTH / 2.0
    gauss = np.exp(-2.0 * np.pi**2 * sigma**2 * mirror**2 / (count * count))
    full = (cas * gauss) @ cas.T / count
    high = full.astype(ml_dtypes.bfloat16)
    low = (full - high.astype(np.float64)).astype(ml_dtypes.bfloat16)
    return high, low


def ring_rows(x_local, count, parts):
    rows = x_local + HALO
    r = np.arange(rows)
    away = np.where(r < x_local + HALO // 2, r, r - rows)
    return np.stack([(part * x_local + away) % count for part in range(parts)])


def look_up(labels_ref, table_ref, out_ref):
    rows, cols = labels_ref.shape
    words = []
    for k in range(table_ref.shape[0] // 4):
        quad = [table_ref[4 * k + b : 4 * k + b + 1, :] for b in range(4)]
        word = quad[0] + quad[1] * 2**8 + quad[2] * 2**16 + lax.shift_left(quad[3], 24)
        words.append(jnp.broadcast_to(word, (rows, LANES)))
    for c in range(cols // LANES):
        lab = labels_ref[:, c * LANES : (c + 1) * LANES]
        lane = lax.bitwise_and(lab, LANES - 1)
        page = lax.shift_right_logical(lab, LANES.bit_length() - 1)
        which = lax.shift_right_logical(page, 2)
        place = lax.bitwise_and(page, 3) * 8
        acc = jnp.take_along_axis(words[0], lane, axis=1)
        for k in range(1, len(words)):
            acc = jnp.where(which == k, jnp.take_along_axis(words[k], lane, axis=1), acc)
        acc = lax.bitwise_and(lax.shift_right_logical(acc, place), 255)
        out_ref[:, c * LANES : (c + 1) * LANES] = acc.astype(jnp.float32).astype(out_ref.dtype)


def gather_kernel(axis, size, labels_ref, table_ref, out_ref, x_ref, send_sem, recv_sem, local_sem):
    me = lax.axis_index(axis)
    chips = size // 2
    chip, core = me // 2, lax.rem(me, 2)
    beside = 2 * chip + 1 - core
    others = [2 * lax.rem(chip + d, chips) + core for d in range(1, chips)]
    barrier = pltpu.get_barrier_semaphore()
    for device in [beside, *others]:
        pl.semaphore_signal(barrier, inc=1, device_id={axis: device}, device_id_type=MESH)
    look_up(labels_ref, table_ref, x_ref)
    local = pltpu.make_async_copy(x_ref, out_ref.at[me], local_sem)
    local.start()
    pl.semaphore_wait(barrier, chips)

    def send(src, slab, device, k):
        copy = pltpu.make_async_remote_copy(
            src_ref=src,
            dst_ref=out_ref.at[slab],
            send_sem=send_sem.at[k],
            recv_sem=recv_sem.at[k],
            device_id={axis: device},
            device_id_type=MESH,
        )
        copy.start()
        return copy

    far = [send(x_ref, me, device, d) for d, device in enumerate(others)]
    near = [send(x_ref, me, beside, chips - 1)]
    for d in range(1, chips):
        far[d - 1].wait_recv()
        slab = 2 * lax.rem(chip + chips - d, chips) + core
        near.append(send(out_ref.at[slab], slab, beside, chips - 1 + d))
    local.wait()
    for copy in far:
        copy.wait_send()
    for copy in near:
        copy.wait()


def gathered_owners(labels, table, axis, size, collective_id):
    return pl.pallas_call(
        functools.partial(gather_kernel, axis, size),
        out_shape=jax.ShapeDtypeStruct((size, *labels.shape), jnp.bfloat16),
        in_specs=[pl.BlockSpec(memory_space=pltpu.VMEM)] * 2,
        out_specs=pl.BlockSpec(memory_space=pltpu.VMEM),
        scratch_shapes=[
            pltpu.VMEM(labels.shape, jnp.bfloat16),
            pltpu.SemaphoreType.DMA((size - 1,)),
            pltpu.SemaphoreType.DMA((size - 1,)),
            pltpu.SemaphoreType.DMA,
        ],
        compiler_params=pltpu.CompilerParams(
            collective_id=collective_id, has_side_effects=True, vmem_limit_bytes=VMEM
        ),
        name="gather_" + axis,
    )(labels, table)


def merge_kernel(axis, size, x_ref, out_ref, recv_ref, send_sem, recv_sem, back_send, back_recv):
    me = lax.axis_index(axis)
    others = [lax.rem(me + k, size) for k in range(1, size)]
    barrier = pltpu.get_barrier_semaphore()
    for device in others:
        pl.semaphore_signal(barrier, inc=1, device_id={axis: device}, device_id_type=MESH)
    pl.semaphore_wait(barrier, size - 1)

    def send(src, dst, sems, k, device):
        copy = pltpu.make_async_remote_copy(
            src_ref=src,
            dst_ref=dst,
            send_sem=sems[0].at[k],
            recv_sem=sems[1].at[k],
            device_id={axis: device},
            device_id_type=MESH,
        )
        copy.start()
        return copy

    there = [
        send(x_ref.at[device], recv_ref.at[k], (send_sem, recv_sem), k, device)
        for k, device in enumerate(others)
    ]
    high, second = x_ref[me, 0], x_ref[me, 1]
    for k in range(size - 1):
        there[k].wait_recv()
        other, third = recv_ref[k, 0], recv_ref[k, 1]
        second = jnp.maximum(jnp.minimum(high, other), jnp.maximum(second, third))
        high = jnp.maximum(high, other)
    out_ref[me, 0] = high
    out_ref[me, 1] = second
    back = [
        send(out_ref.at[me], out_ref.at[me], (back_send, back_recv), k, device)
        for k, device in enumerate(others)
    ]
    for copy in there:
        copy.wait_send()
    for copy in back:
        copy.wait()


def merged(x, axis, size, collective_id):
    return pl.pallas_call(
        functools.partial(merge_kernel, axis, size),
        out_shape=jax.ShapeDtypeStruct(x.shape, x.dtype),
        in_specs=[pl.BlockSpec(memory_space=pltpu.VMEM)],
        out_specs=pl.BlockSpec(memory_space=pltpu.VMEM),
        scratch_shapes=[pltpu.VMEM((size - 1, *x.shape[1:]), x.dtype)]
        + [pltpu.SemaphoreType.DMA((size - 1,))] * 4,
        compiler_params=pltpu.CompilerParams(
            collective_id=collective_id, has_side_effects=True, vmem_limit_bytes=VMEM
        ),
        name="merge_" + axis,
    )(x)


def tile_place(k, per_piece):
    row = 8 * (k % per_piece)
    return k // per_piece, slice(row, row + 8)


def smooth_kernel(
    x_local, fam_local, group,
    owner_ref, mx_ref, my_ref, u_ref, tops_ref, rel_ref, own_ref, t_ref,
):
    step = pl.program_id(0)
    nx, ny = owner_ref.shape
    rows = x_local + HALO
    x0 = lax.axis_index("gx") * x_local
    first = lax.axis_index("fam") * fam_local + step * group

    @pl.when(step == 0)
    def _():
        mine = owner_ref[pl.ds(pl.multiple_of(x0, x_local), x_local), :].astype(jnp.float32)
        after = lax.rem(x0 + x_local, nx)
        before = lax.rem(x0 + nx - 16, nx)
        right = owner_ref[pl.ds(pl.multiple_of(after, 16), 16), :].astype(jnp.float32)[0:HALO]
        left = owner_ref[pl.ds(pl.multiple_of(before, 16), 16), :].astype(jnp.float32)[HALO:16]
        place = lax.broadcasted_iota(jnp.int32, (HALO, ny), 0)
        own_ref[0:x_local, :] = mine
        own_ref[x_local:rows, :] = jnp.where(place < HALO // 2, right, left)
        tops_ref[...] = jnp.full(tops_ref.shape, BIG, jnp.float32)

    shift = jnp.full((nx, ny), first.astype(jnp.float32), jnp.float32).astype(jnp.bfloat16)
    rel_ref[...] = owner_ref[...] - shift
    mx = mx_ref[0]
    for j in range(group):
        chi = jnp.where(
            rel_ref[...] == jnp.bfloat16(j), jnp.bfloat16(1), jnp.bfloat16(0)
        )
        both = jnp.dot(mx, chi, preferred_element_type=jnp.float32)
        t_ref[j * rows : (j + 1) * rows, :] = both[:rows] + both[rows:]
    t = t_ref[...].astype(jnp.bfloat16)
    s = jnp.dot(t, my_ref[0], preferred_element_type=jnp.float32)
    for part in range(1, my_ref.shape[0]):
        s = s + jnp.dot(t, my_ref[part], preferred_element_type=jnp.float32)
    t_ref[...] = s
    base = first.astype(jnp.float32)
    per_piece = tops_ref.shape[2] // 8
    for r in range(rows // 8):
        strip = slice(8 * r, 8 * r + 8)
        for c in range(ny // LANES):
            cols = slice(c * LANES, (c + 1) * LANES)
            piece, place = tile_place(r * (ny // LANES) + c, per_piece)
            own = own_ref[strip, cols] - base
            high, second = tops_ref[piece, 0, place, :], tops_ref[piece, 1, place, :]
            for j in range(group):
                u = t_ref[j * rows + 8 * r : j * rows + 8 * r + 8, cols]
                u = u + jnp.where(own == float(j), fidelity, 0.0)
                u_ref[j, strip, cols] = u
                second = jnp.maximum(second, jnp.minimum(high, u))
                high = jnp.maximum(high, u)
            tops_ref[piece, 0, place, :] = high
            tops_ref[piece, 1, place, :] = second


def smoothed(owner, mx, my, x_local, fam_local, fams):
    nx, ny = owner.shape
    rows = x_local + HALO
    group = min(8, fam_local)
    tiles = rows * ny // (8 * LANES)
    pieces = (fams, 2, 8 * (-(-tiles // fams)), LANES)
    return pl.pallas_call(
        functools.partial(smooth_kernel, x_local, fam_local, group),
        grid=(fam_local // group,),
        out_shape=(
            jax.ShapeDtypeStruct((fam_local, rows, ny), jnp.float32),
            jax.ShapeDtypeStruct(pieces, jnp.float32),
        ),
        in_specs=[
            pl.BlockSpec((nx, ny), lambda i: (0, 0)),
            pl.BlockSpec((1, *mx.shape[1:]), lambda i: (lax.axis_index("gx"), 0, 0)),
            pl.BlockSpec(my.shape, lambda i: (0, 0, 0)),
        ],
        out_specs=(
            pl.BlockSpec((group, rows, ny), lambda i: (i, 0, 0)),
            pl.BlockSpec(pieces, lambda i: (0, 0, 0, 0)),
        ),
        scratch_shapes=[
            pltpu.VMEM((nx, ny), jnp.bfloat16),
            pltpu.VMEM((rows, ny), jnp.float32),
            pltpu.VMEM((group * rows, ny), jnp.float32),
        ],
        compiler_params=pltpu.CompilerParams(vmem_limit_bytes=VMEM),
        name="smooth",
    )(owner, mx, my)


def redistance_kernel(
    x_local, group, tops_ref, u_ref, out_ref, half_ref, first_ref, phi_ref, flag_ref
):
    rows, ny = u_ref.shape[1:]
    chunks = ny // LANES
    strips = rows // 8
    per_piece = tops_ref.shape[2] // 8

    def strip(r):
        return slice(8 * r, 8 * r + 8)

    def chunk(c):
        return slice(c * LANES, (c + 1) * LANES)

    def put(ref, r, c, value):
        ref[c, 8 * r + HALO : 8 * r + HALO + 8, :] = value
        if r == strips - 1:
            ref[c, 0:HALO, :] = value

    peaks = [jnp.full((8, LANES), BIG, jnp.float32) for _ in range(group)]
    for r in range(strips):
        for c in range(chunks):
            piece, place = tile_place(r * chunks + c, per_piece)
            top1, top2 = tops_ref[piece, 0, place, :], tops_ref[piece, 1, place, :]
            for j in range(group):
                u = u_ref[j, strip(r), chunk(c)]
                phi = scale_factor * (u - jnp.where(u >= top1, top2, top1))
                put(first_ref.at[j], r, c, phi)
                half_ref[j, strip(r), chunk(c)] = phi * (step_size * lax.rsqrt(phi * phi + 1.0))
                peaks[j] = jnp.maximum(peaks[j], phi)
    for j in range(group):
        flag_ref[j] = (jnp.max(peaks[j]) > 0.0).astype(jnp.int32)

    lane = lax.broadcasted_iota(jnp.int32, (8, LANES), 1)
    is_first, is_last = lane == 0, lane == LANES - 1

    def sweeps(j, some_positive):
        for sweep in range(SWEEPS):
            if sweep == 0:
                src = first_ref.at[j]
            else:
                src = phi_ref.at[(sweep + 1) % 2]
            dst = phi_ref.at[sweep % 2]

            def load(r, c, shift):
                start = 8 * r + HALO + shift
                if r == strips - 1 and shift > 0:
                    start = shift
                return src[c, start : start + 8, :]

            final = sweep == SWEEPS - 1
            for r in range(x_local // 8 if final else strips):
                mid = [load(r, c, 0) for c in range(chunks)]
                to_right = [pltpu.roll(v, 1, 1) for v in mid]
                to_left = [pltpu.roll(v, LANES - 1, 1) for v in mid]
                for c in range(chunks):
                    half, here = half_ref[j, strip(r), chunk(c)], mid[c]
                    x_low, x_high = load(r, c, -1), load(r, c, 1)
                    y_low = jnp.where(is_first, to_right[c - 1], to_right[c])
                    y_high = jnp.where(is_last, to_left[(c + 1) % chunks], to_left[c])
                    if some_positive:
                        sig = jnp.where(half > 0.0, 1.0, -1.0)
                        size = here * sig
                        gx = size - jnp.minimum(x_low * sig, x_high * sig)
                        gy = size - jnp.minimum(y_low * sig, y_high * sig)
                    else:
                        gx = jnp.maximum(x_low, x_high) - here
                        gy = jnp.maximum(y_low, y_high) - here
                    gx, gy = jnp.maximum(gx, 1e-18), jnp.maximum(gy, 1e-18)
                    square = gx * gx + gy * gy
                    grad = square * lax.rsqrt(square)
                    new = here - half * (grad - 1.0)
                    if final:
                        out_ref[j, strip(r), chunk(c)] = new
                    else:
                        put(dst, r, c, new)

    def one(j, carry):
        @pl.when(flag_ref[j] == 0)
        def _():
            sweeps(j, False)

        @pl.when(flag_ref[j] != 0)
        def _():
            sweeps(j, True)

        return carry

    lax.fori_loop(0, group, one, 0)


def redistanced(tops, u, x_local):
    fam_local, rows, ny = u.shape
    group = min(8, fam_local)
    chunks = ny // LANES
    return pl.pallas_call(
        functools.partial(redistance_kernel, x_local, group),
        grid=(fam_local // group,),
        out_shape=jax.ShapeDtypeStruct((fam_local, x_local, ny), jnp.float32),
        in_specs=[
            pl.BlockSpec(tops.shape, lambda i: (0, 0, 0, 0)),
            pl.BlockSpec((group, rows, ny), lambda i: (i, 0, 0)),
        ],
        out_specs=pl.BlockSpec((group, x_local, ny), lambda i: (i, 0, 0)),
        scratch_shapes=[
            pltpu.VMEM((group, rows, ny), jnp.float32),
            pltpu.VMEM((group, chunks, rows + HALO, LANES), jnp.float32),
            pltpu.VMEM((2, chunks, rows + HALO, LANES), jnp.float32),
            pltpu.SMEM((group,), jnp.int32),
        ],
        compiler_params=pltpu.CompilerParams(vmem_limit_bytes=VMEM),
        name="redistance",
    )(tops, u)


def body(labels, family_of_grain, mx, my):
    parts, fams = lax.axis_size("gx"), lax.axis_size("fam")
    nz, x_local, ny = labels.shape
    assert nz == 1
    nx = x_local * parts
    fam_local = F // fams
    table = family_of_grain.reshape(-1, LANES)
    owner = gathered_owners(labels[0], table, "gx", parts, 0).reshape(nx, ny)
    u, tops = smoothed(owner, mx, my, x_local, fam_local, fams)
    tops = merged(tops, "fam", fams, 1)
    return redistanced(tops, u, x_local)[:, None]


def solution(mesh):
    def run(labels, family_of_grain):
        nz, nx, ny = labels.shape
        parts = mesh.shape["gx"]
        high, low = smoothing(nx)
        rows = ring_rows(nx // parts, nx, parts)
        mx = jnp.asarray(np.concatenate([high[rows], low[rows]], axis=1))
        my = jnp.asarray(smoothing(ny)[0][None])
        mapped = jax.shard_map(
            body,
            mesh=mesh,
            in_specs=(P(None, "gx", None), P(), P(), P()),
            out_specs=P("fam", None, "gx", None),
            check_vma=False,
        )
        return mapped(labels, family_of_grain, mx, my)

    return run
```

```python
import functools

import jax
import jax.numpy as jnp
import ml_dtypes
import numpy as np
from jax import lax
from jax.experimental import pallas as pl
from jax.experimental.pallas import tpu as pltpu
from jax.sharding import PartitionSpec as P

F = 256
WIDTH = 2
SWEEPS = 3
HALO = 8
LANES = 128
BIG = -1e30
VMEM = 60 * 2**20
MESH = pl.DeviceIdType.MESH

fidelity = 0.25
scale_factor = 8.0
step_size = 0.5


def smoothing(count):
    idx = np.arange(count).astype(np.float32)
    angle = (np.float32(2.0 * np.pi) * np.outer(idx, idx)) / np.float32(count)
    cas = (np.cos(angle) + np.sin(angle)).astype(ml_dtypes.bfloat16).astype(np.float64)
    freq = np.arange(count)
    mirror = np.minimum(freq, count - freq).astype(np.float64)
    sigma = WIDTH / 2.0
    gauss = np.exp(-2.0 * np.pi**2 * sigma**2 * mirror**2 / (count * count))
    full = (cas * gauss) @ cas.T / count
    high = full.astype(ml_dtypes.bfloat16)
    low = (full - high.astype(np.float64)).astype(ml_dtypes.bfloat16)
    return high, low


def ring_rows(x_local, count, parts):
    rows = x_local + HALO
    r = np.arange(rows)
    away = np.where(r < x_local + HALO // 2, r, r - rows)
    return np.stack([(part * x_local + away) % count for part in range(parts)])


def look_up(labels_ref, table_ref, out_ref):
    rows, cols = labels_ref.shape
    words = []
    for k in range(table_ref.shape[0] // 4):
        quad = [table_ref[4 * k + b : 4 * k + b + 1, :] for b in range(4)]
        word = quad[0] + quad[1] * 2**8 + quad[2] * 2**16 + lax.shift_left(quad[3], 24)
        words.append(jnp.broadcast_to(word, (rows, LANES)))
    for c in range(cols // LANES):
        lab = labels_ref[:, c * LANES : (c + 1) * LANES]
        lane = lax.bitwise_and(lab, LANES - 1)
        page = lax.shift_right_logical(lab, LANES.bit_length() - 1)
        which = lax.shift_right_logical(page, 2)
        place = lax.bitwise_and(page, 3) * 8
        acc = jnp.take_along_axis(words[0], lane, axis=1)
        for k in range(1, len(words)):
            acc = jnp.where(which == k, jnp.take_along_axis(words[k], lane, axis=1), acc)
        acc = lax.bitwise_and(lax.shift_right_logical(acc, place), 255)
        out_ref[:, c * LANES : (c + 1) * LANES] = acc.astype(jnp.float32).astype(out_ref.dtype)


def gather_kernel(axis, size, labels_ref, table_ref, out_ref, x_ref, send_sem, recv_sem, local_sem):
    me = lax.axis_index(axis)
    chips = size // 2
    chip, core = me // 2, lax.rem(me, 2)
    beside = 2 * chip + 1 - core
    others = [2 * lax.rem(chip + d, chips) + core for d in range(1, chips)]
    barrier = pltpu.get_barrier_semaphore()
    for device in [beside, *others]:
        pl.semaphore_signal(barrier, inc=1, device_id={axis: device}, device_id_type=MESH)
    look_up(labels_ref, table_ref, x_ref)
    local = pltpu.make_async_copy(x_ref, out_ref.at[me], local_sem)
    local.start()
    pl.semaphore_wait(barrier, chips)

    def send(src, slab, device, k):
        copy = pltpu.make_async_remote_copy(
            src_ref=src,
            dst_ref=out_ref.at[slab],
            send_sem=send_sem.at[k],
            recv_sem=recv_sem.at[k],
            device_id={axis: device},
            device_id_type=MESH,
        )
        copy.start()
        return copy

    far = [send(x_ref, me, device, d) for d, device in enumerate(others)]
    near = [send(x_ref, me, beside, chips - 1)]
    for d in range(1, chips):
        far[d - 1].wait_recv()
        slab = 2 * lax.rem(chip + chips - d, chips) + core
        near.append(send(out_ref.at[slab], slab, beside, chips - 1 + d))
    local.wait()
    for copy in far:
        copy.wait_send()
    for copy in near:
        copy.wait()


def gathered_owners(labels, table, axis, size, collective_id):
    return pl.pallas_call(
        functools.partial(gather_kernel, axis, size),
        out_shape=jax.ShapeDtypeStruct((size, *labels.shape), jnp.bfloat16),
        in_specs=[pl.BlockSpec(memory_space=pltpu.VMEM)] * 2,
        out_specs=pl.BlockSpec(memory_space=pltpu.VMEM),
        scratch_shapes=[
            pltpu.VMEM(labels.shape, jnp.bfloat16),
            pltpu.SemaphoreType.DMA((size - 1,)),
            pltpu.SemaphoreType.DMA((size - 1,)),
            pltpu.SemaphoreType.DMA,
        ],
        compiler_params=pltpu.CompilerParams(
            collective_id=collective_id, has_side_effects=True, vmem_limit_bytes=VMEM
        ),
        name="gather_" + axis,
    )(labels, table)


def peers(axis, size):
    me = lax.axis_index(axis)
    return me, [lax.rem(me + k, size) for k in range(1, size)]


def greet(axis, size):
    barrier = pltpu.get_barrier_semaphore()
    for device in peers(axis, size)[1]:
        pl.semaphore_signal(barrier, inc=1, device_id={axis: device}, device_id_type=MESH)


def merge(axis, size, x_ref, out_ref, recv_ref, send_sem, recv_sem, back_send, back_recv):
    me, others = peers(axis, size)
    pl.semaphore_wait(pltpu.get_barrier_semaphore(), size - 1)

    def send(src, dst, sems, k, device):
        copy = pltpu.make_async_remote_copy(
            src_ref=src,
            dst_ref=dst,
            send_sem=sems[0].at[k],
            recv_sem=sems[1].at[k],
            device_id={axis: device},
            device_id_type=MESH,
        )
        copy.start()
        return copy

    there = [
        send(x_ref.at[device], recv_ref.at[k], (send_sem, recv_sem), k, device)
        for k, device in enumerate(others)
    ]
    high, second = x_ref[me, 0], x_ref[me, 1]
    for k in range(size - 1):
        there[k].wait_recv()
        other, third = recv_ref[k, 0], recv_ref[k, 1]
        second = jnp.maximum(jnp.minimum(high, other), jnp.maximum(second, third))
        high = jnp.maximum(high, other)
    out_ref[me, 0] = high
    out_ref[me, 1] = second
    back = [
        send(out_ref.at[me], out_ref.at[me], (back_send, back_recv), k, device)
        for k, device in enumerate(others)
    ]
    for copy in there:
        copy.wait_send()
    for copy in back:
        copy.wait()


def tile_place(k, per_piece):
    row = 8 * (k % per_piece)
    return k // per_piece, slice(row, row + 8)


def smooth_kernel(
    x_local, fam_local, group,
    owner_ref, mx_ref, my_ref, u_ref, all_ref, rel_ref, own_ref, t_ref, tops_ref, *exchange,
):
    step = pl.program_id(0)
    nx, ny = owner_ref.shape
    rows = x_local + HALO
    x0 = lax.axis_index("gx") * x_local
    first = lax.axis_index("fam") * fam_local + step * group

    @pl.when(step == 0)
    def _():
        greet("fam", tops_ref.shape[0])
        mine = owner_ref[pl.ds(pl.multiple_of(x0, x_local), x_local), :].astype(jnp.float32)
        after = lax.rem(x0 + x_local, nx)
        before = lax.rem(x0 + nx - 16, nx)
        right = owner_ref[pl.ds(pl.multiple_of(after, 16), 16), :].astype(jnp.float32)[0:HALO]
        left = owner_ref[pl.ds(pl.multiple_of(before, 16), 16), :].astype(jnp.float32)[HALO:16]
        place = lax.broadcasted_iota(jnp.int32, (HALO, ny), 0)
        own_ref[0:x_local, :] = mine
        own_ref[x_local:rows, :] = jnp.where(place < HALO // 2, right, left)
        tops_ref[...] = jnp.full(tops_ref.shape, BIG, jnp.float32)

    shift = jnp.full((nx, ny), first.astype(jnp.float32), jnp.float32).astype(jnp.bfloat16)
    rel_ref[...] = owner_ref[...] - shift
    mx = mx_ref[0]
    for j in range(group):
        chi = jnp.where(
            rel_ref[...] == jnp.bfloat16(j), jnp.bfloat16(1), jnp.bfloat16(0)
        )
        both = jnp.dot(mx, chi, preferred_element_type=jnp.float32)
        t_ref[j * rows : (j + 1) * rows, :] = both[:rows] + both[rows:]
    t = t_ref[...].astype(jnp.bfloat16)
    s = jnp.dot(t, my_ref[0], preferred_element_type=jnp.float32)
    for part in range(1, my_ref.shape[0]):
        s = s + jnp.dot(t, my_ref[part], preferred_element_type=jnp.float32)
    t_ref[...] = s
    base = first.astype(jnp.float32)
    per_piece = tops_ref.shape[2] // 8
    for r in range(rows // 8):
        strip = slice(8 * r, 8 * r + 8)
        for c in range(ny // LANES):
            cols = slice(c * LANES, (c + 1) * LANES)
            piece, place = tile_place(r * (ny // LANES) + c, per_piece)
            own = own_ref[strip, cols] - base
            high, second = tops_ref[piece, 0, place, :], tops_ref[piece, 1, place, :]
            for j in range(group):
                u = t_ref[j * rows + 8 * r : j * rows + 8 * r + 8, cols]
                u = u + jnp.where(own == float(j), fidelity, 0.0)
                u_ref[j, strip, cols] = u
                second = jnp.maximum(second, jnp.minimum(high, u))
                high = jnp.maximum(high, u)
            tops_ref[piece, 0, place, :] = high
            tops_ref[piece, 1, place, :] = second

    @pl.when(step == pl.num_programs(0) - 1)
    def _():
        merge("fam", tops_ref.shape[0], tops_ref, *exchange)
        all_ref[...] = exchange[0][...]


def smoothed(owner, mx, my, x_local, fam_local, fams):
    nx, ny = owner.shape
    rows = x_local + HALO
    group = min(8, fam_local)
    tiles = rows * ny // (8 * LANES)
    pieces = (fams, 2, 8 * (-(-tiles // fams)), LANES)
    return pl.pallas_call(
        functools.partial(smooth_kernel, x_local, fam_local, group),
        grid=(fam_local // group,),
        out_shape=(
            jax.ShapeDtypeStruct((fam_local, rows, ny), jnp.float32),
            jax.ShapeDtypeStruct(pieces, jnp.float32),
        ),
        in_specs=[
            pl.BlockSpec((nx, ny), lambda i: (0, 0)),
            pl.BlockSpec((1, *mx.shape[1:]), lambda i: (lax.axis_index("gx"), 0, 0)),
            pl.BlockSpec(my.shape, lambda i: (0, 0, 0)),
        ],
        out_specs=(
            pl.BlockSpec((group, rows, ny), lambda i: (i, 0, 0)),
            pl.BlockSpec(pieces, lambda i: (0, 0, 0, 0)),
        ),
        scratch_shapes=[
            pltpu.VMEM((nx, ny), jnp.bfloat16),
            pltpu.VMEM((rows, ny), jnp.float32),
            pltpu.VMEM((group * rows, ny), jnp.float32),
            pltpu.VMEM(pieces, jnp.float32),
            pltpu.VMEM(pieces, jnp.float32),
            pltpu.VMEM((fams - 1, *pieces[1:]), jnp.float32),
        ]
        + [pltpu.SemaphoreType.DMA((fams - 1,))] * 4,
        compiler_params=pltpu.CompilerParams(
            collective_id=1, has_side_effects=True, vmem_limit_bytes=VMEM
        ),
        name="smooth",
    )(owner, mx, my)


def redistance_kernel(x_local, group, tops_ref, u_ref, out_ref, phi_ref, sig_ref, half_ref):
    rows, ny = u_ref.shape[1:]
    chunks = ny // LANES
    strips = rows // 8

    per_piece = tops_ref.shape[2] // 8
    lane = lax.broadcasted_iota(jnp.int32, (8, LANES), 1)
    is_first, is_last = lane == 0, lane == LANES - 1

    def put(slot, r, c, value):
        phi_ref[slot, c, 8 * r + HALO : 8 * r + HALO + 8, :] = value
        if r == strips - 1:
            phi_ref[slot, c, 0:HALO, :] = value

    def one(j, carry):
        for r in range(strips):
            for c in range(chunks):
                rs, cs = slice(8 * r, 8 * r + 8), slice(c * LANES, (c + 1) * LANES)
                u = u_ref[j, rs, cs]
                piece, place = tile_place(r * chunks + c, per_piece)
                top1, top2 = tops_ref[piece, 0, place, :], tops_ref[piece, 1, place, :]
                phi = scale_factor * (u - jnp.where(u >= top1, top2, top1))
                put(0, r, c, phi)
                sig_ref[c, rs, :] = jnp.where(phi > 0.0, 1.0, -1.0)
                half_ref[c, rs, :] = phi * (step_size * lax.rsqrt(phi * phi + 1.0))
        for sweep in range(SWEEPS):
            src, dst = sweep % 2, (sweep + 1) % 2
            final = sweep == SWEEPS - 1
            for r in range(x_local // 8 if final else strips):
                rs = slice(8 * r, 8 * r + 8)
                mid = [phi_ref[src, c, 8 * r + HALO : 8 * r + HALO + 8, :] for c in range(chunks)]
                to_right = [pltpu.roll(v, 1, 1) for v in mid]
                to_left = [pltpu.roll(v, LANES - 1, 1) for v in mid]
                for c in range(chunks):
                    sig, half, centre = sig_ref[c, rs, :], half_ref[c, rs, :], mid[c]
                    y_low = jnp.where(is_first, to_right[c - 1], to_right[c])
                    y_high = jnp.where(is_last, to_left[(c + 1) % chunks], to_left[c])
                    x_low = phi_ref[src, c, 8 * r + HALO - 1 : 8 * r + HALO + 7, :]
                    if r == strips - 1:
                        x_high = phi_ref[src, c, 1:9, :]
                    else:
                        x_high = phi_ref[src, c, 8 * r + HALO + 1 : 8 * r + HALO + 9, :]
                    here = centre * sig
                    gx = jnp.maximum(here - jnp.minimum(x_low * sig, x_high * sig), 1e-18)
                    gy = jnp.maximum(here - jnp.minimum(y_low * sig, y_high * sig), 1e-18)
                    square = gx * gx + gy * gy
                    grad = square * lax.rsqrt(square)
                    new = centre - half * (grad - 1.0)
                    if final:
                        out_ref[j, rs, c * LANES : (c + 1) * LANES] = new
                    else:
                        put(dst, r, c, new)
        return carry

    lax.fori_loop(0, group, one, 0)


def redistanced(tops, u, x_local):
    fam_local, rows, ny = u.shape
    group = min(8, fam_local)
    chunks = ny // LANES
    return pl.pallas_call(
        functools.partial(redistance_kernel, x_local, group),
        grid=(fam_local // group,),
        out_shape=jax.ShapeDtypeStruct((fam_local, x_local, ny), jnp.float32),
        in_specs=[
            pl.BlockSpec(tops.shape, lambda i: (0, 0, 0, 0)),
            pl.BlockSpec((group, rows, ny), lambda i: (i, 0, 0)),
        ],
        out_specs=pl.BlockSpec((group, x_local, ny), lambda i: (i, 0, 0)),
        scratch_shapes=[
            pltpu.VMEM((2, chunks, rows + HALO, LANES), jnp.float32),
            pltpu.VMEM((chunks, rows, LANES), jnp.float32),
            pltpu.VMEM((chunks, rows, LANES), jnp.float32),
        ],
        compiler_params=pltpu.CompilerParams(vmem_limit_bytes=VMEM),
        name="redistance",
    )(tops, u)


def body(labels, family_of_grain, mx, my):
    parts, fams = lax.axis_size("gx"), lax.axis_size("fam")
    nz, x_local, ny = labels.shape
    assert nz == 1
    nx = x_local * parts
    fam_local = F // fams
    table = family_of_grain.reshape(-1, LANES)
    owner = gathered_owners(labels[0], table, "gx", parts, 0).reshape(nx, ny)
    u, tops = smoothed(owner, mx, my, x_local, fam_local, fams)
    return redistanced(tops, u, x_local)[:, None]


def solution(mesh):
    def run(labels, family_of_grain):
        nz, nx, ny = labels.shape
        parts = mesh.shape["gx"]
        high, low = smoothing(nx)
        rows = ring_rows(nx // parts, nx, parts)
        mx = jnp.asarray(np.concatenate([high[rows], low[rows]], axis=1))
        my = jnp.asarray(smoothing(ny)[0][None])
        mapped = jax.shard_map(
            body,
            mesh=mesh,
            in_specs=(P(None, "gx", None), P(), P(), P()),
            out_specs=P("fam", None, "gx", None),
            check_vma=False,
        )
        return mapped(labels, family_of_grain, mx, my)

    return run
```

```python
import functools

import jax
import jax.numpy as jnp
import ml_dtypes
import numpy as np
from jax import lax
from jax.experimental import pallas as pl
from jax.experimental.pallas import tpu as pltpu
from jax.sharding import PartitionSpec as P

F = 256
WIDTH = 2
SWEEPS = 3
HALO = 8
LANES = 128
BIG = -1e30
VMEM = 60 * 2**20
MESH = pl.DeviceIdType.MESH

fidelity = 0.25
scale_factor = 8.0
step_size = 0.5


def smoothing(count):
    idx = np.arange(count).astype(np.float32)
    angle = (np.float32(2.0 * np.pi) * np.outer(idx, idx)) / np.float32(count)
    cas = (np.cos(angle) + np.sin(angle)).astype(ml_dtypes.bfloat16).astype(np.float64)
    freq = np.arange(count)
    mirror = np.minimum(freq, count - freq).astype(np.float64)
    sigma = WIDTH / 2.0
    gauss = np.exp(-2.0 * np.pi**2 * sigma**2 * mirror**2 / (count * count))
    full = (cas * gauss) @ cas.T / count
    high = full.astype(ml_dtypes.bfloat16)
    low = (full - high.astype(np.float64)).astype(ml_dtypes.bfloat16)
    return high, low


def ring_rows(x_local, count, parts):
    rows = x_local + HALO
    r = np.arange(rows)
    away = np.where(r < x_local + HALO // 2, r, r - rows)
    return np.stack([(part * x_local + away) % count for part in range(parts)])


def spread_columns(count):
    place = np.arange(count)
    spread = (place % LANES) * (count // LANES) + place // LANES
    to_spread = (np.arange(count)[:, None] == spread[None]).astype(ml_dtypes.bfloat16)
    return spread, to_spread


def look_up(labels_ref, table_ref, out_ref):
    rows, cols = labels_ref.shape
    words = []
    for k in range(table_ref.shape[0] // 4):
        quad = [table_ref[4 * k + b : 4 * k + b + 1, :] for b in range(4)]
        word = quad[0] + quad[1] * 2**8 + quad[2] * 2**16 + lax.shift_left(quad[3], 24)
        words.append(jnp.broadcast_to(word, (rows, LANES)))
    for c in range(cols // LANES):
        lab = labels_ref[:, c * LANES : (c + 1) * LANES]
        lane = lax.bitwise_and(lab, LANES - 1)
        page = lax.shift_right_logical(lab, LANES.bit_length() - 1)
        which = lax.shift_right_logical(page, 2)
        place = lax.bitwise_and(page, 3) * 8
        acc = jnp.take_along_axis(words[0], lane, axis=1)
        for k in range(1, len(words)):
            acc = jnp.where(which == k, jnp.take_along_axis(words[k], lane, axis=1), acc)
        acc = lax.bitwise_and(lax.shift_right_logical(acc, place), 255)
        out_ref[:, c * LANES : (c + 1) * LANES] = acc.astype(jnp.float32).astype(out_ref.dtype)


def gather_kernel(axis, size, labels_ref, table_ref, out_ref, x_ref, send_sem, recv_sem, local_sem):
    me = lax.axis_index(axis)
    chips = size // 2
    chip, core = me // 2, lax.rem(me, 2)
    beside = 2 * chip + 1 - core
    others = [2 * lax.rem(chip + d, chips) + core for d in range(1, chips)]
    barrier = pltpu.get_barrier_semaphore()
    for device in [beside, *others]:
        pl.semaphore_signal(barrier, inc=1, device_id={axis: device}, device_id_type=MESH)
    look_up(labels_ref, table_ref, x_ref)
    local = pltpu.make_async_copy(x_ref, out_ref.at[me], local_sem)
    local.start()
    pl.semaphore_wait(barrier, chips)

    def send(src, slab, device, k):
        copy = pltpu.make_async_remote_copy(
            src_ref=src,
            dst_ref=out_ref.at[slab],
            send_sem=send_sem.at[k],
            recv_sem=recv_sem.at[k],
            device_id={axis: device},
            device_id_type=MESH,
        )
        copy.start()
        return copy

    far = [send(x_ref, me, device, d) for d, device in enumerate(others)]
    near = [send(x_ref, me, beside, chips - 1)]
    for d in range(1, chips):
        far[d - 1].wait_recv()
        slab = 2 * lax.rem(chip + chips - d, chips) + core
        near.append(send(out_ref.at[slab], slab, beside, chips - 1 + d))
    local.wait()
    for copy in far:
        copy.wait_send()
    for copy in near:
        copy.wait()


def gathered_owners(labels, table, axis, size, collective_id):
    return pl.pallas_call(
        functools.partial(gather_kernel, axis, size),
        out_shape=jax.ShapeDtypeStruct((size, *labels.shape), jnp.bfloat16),
        in_specs=[pl.BlockSpec(memory_space=pltpu.VMEM)] * 2,
        out_specs=pl.BlockSpec(memory_space=pltpu.VMEM),
        scratch_shapes=[
            pltpu.VMEM(labels.shape, jnp.bfloat16),
            pltpu.SemaphoreType.DMA((size - 1,)),
            pltpu.SemaphoreType.DMA((size - 1,)),
            pltpu.SemaphoreType.DMA,
        ],
        compiler_params=pltpu.CompilerParams(
            collective_id=collective_id, has_side_effects=True, vmem_limit_bytes=VMEM
        ),
        name="gather_" + axis,
    )(labels, table)


def peers(axis, size):
    me = lax.axis_index(axis)
    return me, [lax.rem(me + k, size) for k in range(1, size)]


def greet(axis, size):
    barrier = pltpu.get_barrier_semaphore()
    for device in peers(axis, size)[1]:
        pl.semaphore_signal(barrier, inc=1, device_id={axis: device}, device_id_type=MESH)


def merge(axis, size, x_ref, out_ref, recv_ref, send_sem, recv_sem, back_send, back_recv):
    me, others = peers(axis, size)
    pl.semaphore_wait(pltpu.get_barrier_semaphore(), size - 1)

    def send(src, dst, sems, k, device):
        copy = pltpu.make_async_remote_copy(
            src_ref=src,
            dst_ref=dst,
            send_sem=sems[0].at[k],
            recv_sem=sems[1].at[k],
            device_id={axis: device},
            device_id_type=MESH,
        )
        copy.start()
        return copy

    there = [
        send(x_ref.at[device], recv_ref.at[k], (send_sem, recv_sem), k, device)
        for k, device in enumerate(others)
    ]
    high, second = x_ref[me, 0], x_ref[me, 1]
    for k in range(size - 1):
        there[k].wait_recv()
        other, third = recv_ref[k, 0], recv_ref[k, 1]
        second = jnp.maximum(jnp.minimum(high, other), jnp.maximum(second, third))
        high = jnp.maximum(high, other)
    out_ref[me, 0] = high
    out_ref[me, 1] = second
    back = [
        send(out_ref.at[me], out_ref.at[me], (back_send, back_recv), k, device)
        for k, device in enumerate(others)
    ]
    for copy in there:
        copy.wait_send()
    for copy in back:
        copy.wait()


def tile_place(k, per_piece):
    row = 8 * (k % per_piece)
    return k // per_piece, slice(row, row + 8)


def smooth_kernel(
    x_local, fam_local, group,
    owner_ref, mx_ref, my_ref, spread_ref, u_ref, all_ref, rel_ref, own_ref, t_ref, tops_ref, *exchange,
):
    step = pl.program_id(0)
    nx, ny = owner_ref.shape
    rows = x_local + HALO
    x0 = lax.axis_index("gx") * x_local
    first = lax.axis_index("fam") * fam_local + step * group

    @pl.when(step == 0)
    def _():
        greet("fam", tops_ref.shape[0])
        mine = owner_ref[pl.ds(pl.multiple_of(x0, x_local), x_local), :].astype(jnp.float32)
        after = lax.rem(x0 + x_local, nx)
        before = lax.rem(x0 + nx - 16, nx)
        right = owner_ref[pl.ds(pl.multiple_of(after, 16), 16), :].astype(jnp.float32)[0:HALO]
        left = owner_ref[pl.ds(pl.multiple_of(before, 16), 16), :].astype(jnp.float32)[HALO:16]
        place = lax.broadcasted_iota(jnp.int32, (HALO, ny), 0)
        own_ref[0:x_local, :] = mine
        own_ref[x_local:rows, :] = jnp.where(place < HALO // 2, right, left)
        own_ref[...] = jnp.dot(
            own_ref[...].astype(jnp.bfloat16), spread_ref[...], preferred_element_type=jnp.float32
        )
        tops_ref[...] = jnp.full(tops_ref.shape, BIG, jnp.float32)

    shift = jnp.full((nx, ny), first.astype(jnp.float32), jnp.float32).astype(jnp.bfloat16)
    rel_ref[...] = owner_ref[...] - shift
    mx = mx_ref[0]
    for j in range(group):
        chi = jnp.where(
            rel_ref[...] == jnp.bfloat16(j), jnp.bfloat16(1), jnp.bfloat16(0)
        )
        both = jnp.dot(mx, chi, preferred_element_type=jnp.float32)
        t_ref[j * rows : (j + 1) * rows, :] = both[:rows] + both[rows:]
    t = t_ref[...].astype(jnp.bfloat16)
    s = jnp.dot(t, my_ref[0], preferred_element_type=jnp.float32)
    for part in range(1, my_ref.shape[0]):
        s = s + jnp.dot(t, my_ref[part], preferred_element_type=jnp.float32)
    t_ref[...] = s
    base = first.astype(jnp.float32)
    per_piece = tops_ref.shape[2] // 8
    for r in range(rows // 8):
        strip = slice(8 * r, 8 * r + 8)
        for c in range(ny // LANES):
            cols = slice(c * LANES, (c + 1) * LANES)
            piece, place = tile_place(r * (ny // LANES) + c, per_piece)
            own = own_ref[strip, cols] - base
            high, second = tops_ref[piece, 0, place, :], tops_ref[piece, 1, place, :]
            for j in range(group):
                u = t_ref[j * rows + 8 * r : j * rows + 8 * r + 8, cols]
                u = u + jnp.where(own == float(j), fidelity, 0.0)
                u_ref[j, strip, cols] = u
                second = jnp.maximum(second, jnp.minimum(high, u))
                high = jnp.maximum(high, u)
            tops_ref[piece, 0, place, :] = high
            tops_ref[piece, 1, place, :] = second

    @pl.when(step == pl.num_programs(0) - 1)
    def _():
        merge("fam", tops_ref.shape[0], tops_ref, *exchange)
        all_ref[...] = exchange[0][...]


def smoothed(owner, mx, my, spread, x_local, fam_local, fams):
    nx, ny = owner.shape
    rows = x_local + HALO
    group = min(8, fam_local)
    tiles = rows * ny // (8 * LANES)
    pieces = (fams, 2, 8 * (-(-tiles // fams)), LANES)
    return pl.pallas_call(
        functools.partial(smooth_kernel, x_local, fam_local, group),
        grid=(fam_local // group,),
        out_shape=(
            jax.ShapeDtypeStruct((fam_local, rows, ny), jnp.float32),
            jax.ShapeDtypeStruct(pieces, jnp.float32),
        ),
        in_specs=[
            pl.BlockSpec((nx, ny), lambda i: (0, 0)),
            pl.BlockSpec((1, *mx.shape[1:]), lambda i: (lax.axis_index("gx"), 0, 0)),
            pl.BlockSpec(my.shape, lambda i: (0, 0, 0)),
            pl.BlockSpec(spread.shape, lambda i: (0, 0)),
        ],
        out_specs=(
            pl.BlockSpec((group, rows, ny), lambda i: (i, 0, 0)),
            pl.BlockSpec(pieces, lambda i: (0, 0, 0, 0)),
        ),
        scratch_shapes=[
            pltpu.VMEM((nx, ny), jnp.bfloat16),
            pltpu.VMEM((rows, ny), jnp.float32),
            pltpu.VMEM((group * rows, ny), jnp.float32),
            pltpu.VMEM(pieces, jnp.float32),
            pltpu.VMEM(pieces, jnp.float32),
            pltpu.VMEM((fams - 1, *pieces[1:]), jnp.float32),
        ]
        + [pltpu.SemaphoreType.DMA((fams - 1,))] * 4,
        compiler_params=pltpu.CompilerParams(
            collective_id=1, has_side_effects=True, vmem_limit_bytes=VMEM
        ),
        name="smooth",
    )(owner, mx, my, spread)


def redistance_kernel(
    x_local, group, tops_ref, u_ref, back_ref, out_ref, phi_ref, sig_ref, half_ref, done_ref
):
    rows, ny = u_ref.shape[1:]
    chunks = ny // LANES
    strips = rows // 8

    per_piece = tops_ref.shape[2] // 8
    def put_back(j):
        done = done_ref[...]
        high = done.astype(jnp.bfloat16)
        low = (done - high.astype(jnp.float32)).astype(jnp.bfloat16)
        both = jnp.concatenate([high, low], axis=0)
        both = jnp.dot(both, back_ref[...], preferred_element_type=jnp.float32)
        out_ref[j] = both[:x_local] + both[x_local:]

    def put(slot, r, c, value):
        phi_ref[slot, c, 8 * r + HALO : 8 * r + HALO + 8, :] = value
        if r == strips - 1:
            phi_ref[slot, c, 0:HALO, :] = value

    def one(j, carry):
        put_back(jnp.maximum(j - 1, 0))
        for r in range(strips):
            for c in range(chunks):
                rs, cs = slice(8 * r, 8 * r + 8), slice(c * LANES, (c + 1) * LANES)
                u = u_ref[j, rs, cs]
                piece, place = tile_place(r * chunks + c, per_piece)
                top1, top2 = tops_ref[piece, 0, place, :], tops_ref[piece, 1, place, :]
                phi = scale_factor * (u - jnp.where(u >= top1, top2, top1))
                put(0, r, c, phi)
                sig_ref[c, rs, :] = jnp.where(phi > 0.0, 1.0, -1.0)
                half_ref[c, rs, :] = phi * (step_size * lax.rsqrt(phi * phi + 1.0))
        for sweep in range(SWEEPS):
            src, dst = sweep % 2, (sweep + 1) % 2
            final = sweep == SWEEPS - 1
            for r in range(x_local // 8 if final else strips):
                rs = slice(8 * r, 8 * r + 8)
                mid = [phi_ref[src, c, 8 * r + HALO : 8 * r + HALO + 8, :] for c in range(chunks)]
                around = [pltpu.roll(mid[-1], 1, 1), *mid, pltpu.roll(mid[0], LANES - 1, 1)]
                for c in range(chunks):
                    sig, half, centre = sig_ref[c, rs, :], half_ref[c, rs, :], mid[c]
                    y_low, y_high = around[c], around[c + 2]
                    x_low = phi_ref[src, c, 8 * r + HALO - 1 : 8 * r + HALO + 7, :]
                    if r == strips - 1:
                        x_high = phi_ref[src, c, 1:9, :]
                    else:
                        x_high = phi_ref[src, c, 8 * r + HALO + 1 : 8 * r + HALO + 9, :]
                    here = centre * sig
                    gx = jnp.maximum(here - jnp.minimum(x_low * sig, x_high * sig), 1e-18)
                    gy = jnp.maximum(here - jnp.minimum(y_low * sig, y_high * sig), 1e-18)
                    square = gx * gx + gy * gy
                    grad = square * lax.rsqrt(square)
                    new = centre - half * (grad - 1.0)
                    if final:
                        done_ref[rs, c * LANES : (c + 1) * LANES] = new
                    else:
                        put(dst, r, c, new)
        return carry

    lax.fori_loop(0, group, one, 0)
    put_back(group - 1)


def redistanced(tops, u, back, x_local):
    fam_local, rows, ny = u.shape
    group = min(8, fam_local)
    chunks = ny // LANES
    return pl.pallas_call(
        functools.partial(redistance_kernel, x_local, group),
        grid=(fam_local // group,),
        out_shape=jax.ShapeDtypeStruct((fam_local, x_local, ny), jnp.float32),
        in_specs=[
            pl.BlockSpec(tops.shape, lambda i: (0, 0, 0, 0)),
            pl.BlockSpec((group, rows, ny), lambda i: (i, 0, 0)),
            pl.BlockSpec(back.shape, lambda i: (0, 0)),
        ],
        out_specs=pl.BlockSpec((group, x_local, ny), lambda i: (i, 0, 0)),
        scratch_shapes=[
            pltpu.VMEM((2, chunks, rows + HALO, LANES), jnp.float32),
            pltpu.VMEM((chunks, rows, LANES), jnp.float32),
            pltpu.VMEM((chunks, rows, LANES), jnp.float32),
            pltpu.VMEM((x_local, ny), jnp.float32),
        ],
        compiler_params=pltpu.CompilerParams(vmem_limit_bytes=VMEM),
        name="redistance",
    )(tops, u, back)


def body(labels, family_of_grain, mx, my, spread, back):
    parts, fams = lax.axis_size("gx"), lax.axis_size("fam")
    nz, x_local, ny = labels.shape
    assert nz == 1
    nx = x_local * parts
    fam_local = F // fams
    table = family_of_grain.reshape(-1, LANES)
    owner = gathered_owners(labels[0], table, "gx", parts, 0).reshape(nx, ny)
    u, tops = smoothed(owner, mx, my, spread, x_local, fam_local, fams)
    return redistanced(tops, u, back, x_local)[:, None]


def solution(mesh):
    def run(labels, family_of_grain):
        nz, nx, ny = labels.shape
        parts = mesh.shape["gx"]
        high, low = smoothing(nx)
        rows = ring_rows(nx // parts, nx, parts)
        mx = jnp.asarray(np.concatenate([high[rows], low[rows]], axis=1))
        order, spread = spread_columns(ny)
        my = jnp.asarray(smoothing(ny)[0][None, :, order])
        mapped = jax.shard_map(
            body,
            mesh=mesh,
            in_specs=(P(None, "gx", None), P(), P(), P(), P(), P()),
            out_specs=P("fam", None, "gx", None),
            check_vma=False,
        )
        return mapped(
            labels, family_of_grain, mx, my, jnp.asarray(spread), jnp.asarray(spread.T)
        )

    return run
```

```python
import functools

import jax
import jax.numpy as jnp
import ml_dtypes
import numpy as np
from jax import lax
from jax.experimental import pallas as pl
from jax.experimental.pallas import tpu as pltpu
from jax.sharding import PartitionSpec as P

F = 256
WIDTH = 2
SWEEPS = 3
HALO = 8
LANES = 128
BIG = -1e30
VMEM = 60 * 2**20
MESH = pl.DeviceIdType.MESH

fidelity = 0.25
scale_factor = 8.0
step_size = 0.5


def smoothing(count):
    idx = np.arange(count).astype(np.float32)
    angle = (np.float32(2.0 * np.pi) * np.outer(idx, idx)) / np.float32(count)
    cas = (np.cos(angle) + np.sin(angle)).astype(ml_dtypes.bfloat16).astype(np.float64)
    freq = np.arange(count)
    mirror = np.minimum(freq, count - freq).astype(np.float64)
    sigma = WIDTH / 2.0
    gauss = np.exp(-2.0 * np.pi**2 * sigma**2 * mirror**2 / (count * count))
    full = (cas * gauss) @ cas.T / count
    high = full.astype(ml_dtypes.bfloat16)
    low = (full - high.astype(np.float64)).astype(ml_dtypes.bfloat16)
    return high, low


def ring_rows(x_local, count, parts):
    rows = x_local + HALO
    r = np.arange(rows)
    away = np.where(r < x_local + HALO // 2, r, r - rows)
    return np.stack([(part * x_local + away) % count for part in range(parts)])


def look_up(labels_ref, table_ref, out_ref):
    rows, cols = labels_ref.shape
    words = []
    for k in range(table_ref.shape[0] // 4):
        quad = [table_ref[4 * k + b : 4 * k + b + 1, :] for b in range(4)]
        word = quad[0] + quad[1] * 2**8 + quad[2] * 2**16 + lax.shift_left(quad[3], 24)
        words.append(jnp.broadcast_to(word, (rows, LANES)))
    for c in range(cols // LANES):
        lab = labels_ref[:, c * LANES : (c + 1) * LANES]
        lane = lax.bitwise_and(lab, LANES - 1)
        page = lax.shift_right_logical(lab, LANES.bit_length() - 1)
        which = lax.shift_right_logical(page, 2)
        place = lax.bitwise_and(page, 3) * 8
        acc = jnp.take_along_axis(words[0], lane, axis=1)
        for k in range(1, len(words)):
            acc = jnp.where(which == k, jnp.take_along_axis(words[k], lane, axis=1), acc)
        acc = lax.bitwise_and(lax.shift_right_logical(acc, place), 255)
        out_ref[:, c * LANES : (c + 1) * LANES] = acc.astype(jnp.float32).astype(out_ref.dtype)


def gather_kernel(axis, size, labels_ref, table_ref, out_ref, x_ref, send_sem, recv_sem, local_sem):
    me = lax.axis_index(axis)
    chips = size // 2
    chip, core = me // 2, lax.rem(me, 2)
    beside = 2 * chip + 1 - core
    others = [2 * lax.rem(chip + d, chips) + core for d in range(1, chips)]
    barrier = pltpu.get_barrier_semaphore()
    for device in [beside, *others]:
        pl.semaphore_signal(barrier, inc=1, device_id={axis: device}, device_id_type=MESH)
    look_up(labels_ref, table_ref, x_ref)
    local = pltpu.make_async_copy(x_ref, out_ref.at[me], local_sem)
    local.start()
    pl.semaphore_wait(barrier, chips)

    def send(src, slab, device, k):
        copy = pltpu.make_async_remote_copy(
            src_ref=src,
            dst_ref=out_ref.at[slab],
            send_sem=send_sem.at[k],
            recv_sem=recv_sem.at[k],
            device_id={axis: device},
            device_id_type=MESH,
        )
        copy.start()
        return copy

    far = [send(x_ref, me, device, d) for d, device in enumerate(others)]
    near = [send(x_ref, me, beside, chips - 1)]
    for d in range(1, chips):
        far[d - 1].wait_recv()
        slab = 2 * lax.rem(chip + chips - d, chips) + core
        near.append(send(out_ref.at[slab], slab, beside, chips - 1 + d))
    local.wait()
    for copy in far:
        copy.wait_send()
    for copy in near:
        copy.wait()


def gathered_owners(labels, table, axis, size, collective_id):
    return pl.pallas_call(
        functools.partial(gather_kernel, axis, size),
        out_shape=jax.ShapeDtypeStruct((size, *labels.shape), jnp.bfloat16),
        in_specs=[pl.BlockSpec(memory_space=pltpu.VMEM)] * 2,
        out_specs=pl.BlockSpec(memory_space=pltpu.VMEM),
        scratch_shapes=[
            pltpu.VMEM(labels.shape, jnp.bfloat16),
            pltpu.SemaphoreType.DMA((size - 1,)),
            pltpu.SemaphoreType.DMA((size - 1,)),
            pltpu.SemaphoreType.DMA,
        ],
        compiler_params=pltpu.CompilerParams(
            collective_id=collective_id, has_side_effects=True, vmem_limit_bytes=VMEM
        ),
        name="gather_" + axis,
    )(labels, table)


def peers(axis, size):
    me = lax.axis_index(axis)
    return me, [lax.rem(me + k, size) for k in range(1, size)]


def greet(axis, size):
    barrier = pltpu.get_barrier_semaphore()
    for device in peers(axis, size)[1]:
        pl.semaphore_signal(barrier, inc=1, device_id={axis: device}, device_id_type=MESH)


def merge(axis, size, x_ref, out_ref, recv_ref, send_sem, recv_sem, back_send, back_recv):
    me, others = peers(axis, size)
    pl.semaphore_wait(pltpu.get_barrier_semaphore(), size - 1)

    def send(src, dst, sems, k, device):
        copy = pltpu.make_async_remote_copy(
            src_ref=src,
            dst_ref=dst,
            send_sem=sems[0].at[k],
            recv_sem=sems[1].at[k],
            device_id={axis: device},
            device_id_type=MESH,
        )
        copy.start()
        return copy

    there = [
        send(x_ref.at[device], recv_ref.at[k], (send_sem, recv_sem), k, device)
        for k, device in enumerate(others)
    ]
    high, second = x_ref[me, 0], x_ref[me, 1]
    for k in range(size - 1):
        there[k].wait_recv()
        other, third = recv_ref[k, 0], recv_ref[k, 1]
        second = jnp.maximum(jnp.minimum(high, other), jnp.maximum(second, third))
        high = jnp.maximum(high, other)
    out_ref[me, 0] = high
    out_ref[me, 1] = second
    back = [
        send(out_ref.at[me], out_ref.at[me], (back_send, back_recv), k, device)
        for k, device in enumerate(others)
    ]
    for copy in there:
        copy.wait_send()
    for copy in back:
        copy.wait()


def tile_place(k, per_piece):
    row = 8 * (k % per_piece)
    return k // per_piece, slice(row, row + 8)


def smooth_kernel(
    x_local, fam_local, group,
    owner_ref, mx_ref, my_ref, u_ref, all_ref, rel_ref, own_ref, t_ref, tops_ref, *exchange,
):
    step = pl.program_id(0)
    nx, ny = owner_ref.shape
    rows = x_local + HALO
    x0 = lax.axis_index("gx") * x_local
    first = lax.axis_index("fam") * fam_local + step * group

    @pl.when(step == 0)
    def _():
        greet("fam", tops_ref.shape[0])
        mine = owner_ref[pl.ds(pl.multiple_of(x0, x_local), x_local), :].astype(jnp.float32)
        after = lax.rem(x0 + x_local, nx)
        before = lax.rem(x0 + nx - 16, nx)
        right = owner_ref[pl.ds(pl.multiple_of(after, 16), 16), :].astype(jnp.float32)[0:HALO]
        left = owner_ref[pl.ds(pl.multiple_of(before, 16), 16), :].astype(jnp.float32)[HALO:16]
        place = lax.broadcasted_iota(jnp.int32, (HALO, ny), 0)
        own_ref[0:x_local, :] = mine
        own_ref[x_local:rows, :] = jnp.where(place < HALO // 2, right, left)
        tops_ref[...] = jnp.full(tops_ref.shape, BIG, jnp.float32)

    shift = jnp.full((nx, ny), first.astype(jnp.float32), jnp.float32).astype(jnp.bfloat16)
    rel_ref[...] = owner_ref[...] - shift
    mx = mx_ref[0]
    for j in range(group):
        chi = jnp.where(
            rel_ref[...] == jnp.bfloat16(j), jnp.bfloat16(1), jnp.bfloat16(0)
        )
        both = jnp.dot(mx, chi, preferred_element_type=jnp.float32)
        t_ref[j * rows : (j + 1) * rows, :] = both[:rows] + both[rows:]
    t = t_ref[...].astype(jnp.bfloat16)
    s = jnp.dot(t, my_ref[0], preferred_element_type=jnp.float32)
    for part in range(1, my_ref.shape[0]):
        s = s + jnp.dot(t, my_ref[part], preferred_element_type=jnp.float32)
    t_ref[...] = s
    base = first.astype(jnp.float32)
    per_piece = tops_ref.shape[2] // 8
    for r in range(rows // 8):
        strip = slice(8 * r, 8 * r + 8)
        for c in range(ny // LANES):
            cols = slice(c * LANES, (c + 1) * LANES)
            piece, place = tile_place(r * (ny // LANES) + c, per_piece)
            own = own_ref[strip, cols] - base
            high, second = tops_ref[piece, 0, place, :], tops_ref[piece, 1, place, :]
            for j in range(group):
                u = t_ref[j * rows + 8 * r : j * rows + 8 * r + 8, cols]
                u = u + jnp.where(own == float(j), fidelity, 0.0)
                u_ref[j, strip, cols] = u
                second = jnp.maximum(second, jnp.minimum(high, u))
                high = jnp.maximum(high, u)
            tops_ref[piece, 0, place, :] = high
            tops_ref[piece, 1, place, :] = second

    @pl.when(step == pl.num_programs(0) - 1)
    def _():
        merge("fam", tops_ref.shape[0], tops_ref, *exchange)
        all_ref[...] = exchange[0][...]


def smoothed(owner, mx, my, x_local, fam_local, fams):
    nx, ny = owner.shape
    rows = x_local + HALO
    group = min(8, fam_local)
    tiles = rows * ny // (8 * LANES)
    pieces = (fams, 2, 8 * (-(-tiles // fams)), LANES)
    return pl.pallas_call(
        functools.partial(smooth_kernel, x_local, fam_local, group),
        grid=(fam_local // group,),
        out_shape=(
            jax.ShapeDtypeStruct((fam_local, rows, ny), jnp.float32),
            jax.ShapeDtypeStruct(pieces, jnp.float32),
        ),
        in_specs=[
            pl.BlockSpec((nx, ny), lambda i: (0, 0)),
            pl.BlockSpec((1, *mx.shape[1:]), lambda i: (lax.axis_index("gx"), 0, 0)),
            pl.BlockSpec(my.shape, lambda i: (0, 0, 0)),
        ],
        out_specs=(
            pl.BlockSpec((group, rows, ny), lambda i: (i, 0, 0)),
            pl.BlockSpec(pieces, lambda i: (0, 0, 0, 0)),
        ),
        scratch_shapes=[
            pltpu.VMEM((nx, ny), jnp.bfloat16),
            pltpu.VMEM((rows, ny), jnp.float32),
            pltpu.VMEM((group * rows, ny), jnp.float32),
            pltpu.VMEM(pieces, jnp.float32),
            pltpu.VMEM(pieces, jnp.float32),
            pltpu.VMEM((fams - 1, *pieces[1:]), jnp.float32),
        ]
        + [pltpu.SemaphoreType.DMA((fams - 1,))] * 4,
        compiler_params=pltpu.CompilerParams(
            collective_id=1, has_side_effects=True, vmem_limit_bytes=VMEM
        ),
        name="smooth",
    )(owner, mx, my)


def redistance_kernel(
    x_local, group, tops_ref, u_ref, out_ref, half_ref, first_ref, phi_ref
):
    rows, ny = u_ref.shape[1:]
    chunks = ny // LANES
    strips = rows // 8
    per_piece = tops_ref.shape[2] // 8

    def strip(r):
        return slice(8 * r, 8 * r + 8)

    def chunk(c):
        return slice(c * LANES, (c + 1) * LANES)

    def put(ref, r, c, value):
        ref[c, 8 * r + HALO : 8 * r + HALO + 8, :] = value
        if r == strips - 1:
            ref[c, 0:HALO, :] = value

    peaks = [jnp.full((8, LANES), BIG, jnp.float32) for _ in range(group)]
    for r in range(strips):
        for c in range(chunks):
            piece, place = tile_place(r * chunks + c, per_piece)
            top1, top2 = tops_ref[piece, 0, place, :], tops_ref[piece, 1, place, :]
            for j in range(group):
                u = u_ref[j, strip(r), chunk(c)]
                phi = scale_factor * (u - jnp.where(u >= top1, top2, top1))
                put(first_ref.at[j], r, c, phi)
                half_ref[j, strip(r), chunk(c)] = phi * (step_size * lax.rsqrt(phi * phi + 1.0))
                peaks[j] = jnp.maximum(peaks[j], phi)
    family = lax.broadcasted_iota(jnp.int32, (8, LANES), 0)
    peak = jnp.full((8, LANES), BIG, jnp.float32)
    for j in range(group):
        highest = jnp.max(peaks[j], axis=0, keepdims=True)
        peak = jnp.where(family == j, jnp.broadcast_to(highest, peak.shape), peak)
    bit = lax.shift_left(jnp.ones_like(family), family).astype(jnp.float32)
    peak = jnp.broadcast_to(jnp.max(peak, axis=1, keepdims=True), peak.shape)
    some = jnp.sum(jnp.where(peak > 0.0, bit, 0.0), axis=0, keepdims=True)
    flags = jnp.max(some).astype(jnp.int32)

    lane = lax.broadcasted_iota(jnp.int32, (8, LANES), 1)
    is_first, is_last = lane == 0, lane == LANES - 1

    def sweeps(j, some_positive):
        for sweep in range(SWEEPS):
            if sweep == 0:
                src = first_ref.at[j]
            else:
                src = phi_ref.at[(sweep + 1) % 2]
            dst = phi_ref.at[sweep % 2]

            def load(r, c, shift):
                start = 8 * r + HALO + shift
                if r == strips - 1 and shift > 0:
                    start = shift
                return src[c, start : start + 8, :]

            final = sweep == SWEEPS - 1
            for r in range(x_local // 8 if final else strips):
                mid = [load(r, c, 0) for c in range(chunks)]
                to_right = [pltpu.roll(v, 1, 1) for v in mid]
                to_left = [pltpu.roll(v, LANES - 1, 1) for v in mid]
                for c in range(chunks):
                    half, here = half_ref[j, strip(r), chunk(c)], mid[c]
                    x_low, x_high = load(r, c, -1), load(r, c, 1)
                    y_low = jnp.where(is_first, to_right[c - 1], to_right[c])
                    y_high = jnp.where(is_last, to_left[(c + 1) % chunks], to_left[c])
                    if some_positive:
                        sig = jnp.where(half > 0.0, 1.0, -1.0)
                        size = here * sig
                        gx = size - jnp.minimum(x_low * sig, x_high * sig)
                        gy = size - jnp.minimum(y_low * sig, y_high * sig)
                    else:
                        gx = jnp.maximum(x_low, x_high) - here
                        gy = jnp.maximum(y_low, y_high) - here
                    gx, gy = jnp.maximum(gx, 1e-18), jnp.maximum(gy, 1e-18)
                    square = gx * gx + gy * gy
                    grad = square * lax.rsqrt(square)
                    new = here - half * (grad - 1.0)
                    if final:
                        out_ref[j, strip(r), chunk(c)] = new
                    else:
                        put(dst, r, c, new)

    def one(j, carry):
        flag = lax.bitwise_and(lax.shift_right_logical(flags, j), 1)

        @pl.when(flag == 0)
        def _():
            sweeps(j, False)

        @pl.when(flag != 0)
        def _():
            sweeps(j, True)

        return carry

    lax.fori_loop(0, group, one, 0)


def redistanced(tops, u, x_local):
    fam_local, rows, ny = u.shape
    group = min(8, fam_local)
    chunks = ny // LANES
    return pl.pallas_call(
        functools.partial(redistance_kernel, x_local, group),
        grid=(fam_local // group,),
        out_shape=jax.ShapeDtypeStruct((fam_local, x_local, ny), jnp.float32),
        in_specs=[
            pl.BlockSpec(tops.shape, lambda i: (0, 0, 0, 0)),
            pl.BlockSpec((group, rows, ny), lambda i: (i, 0, 0)),
        ],
        out_specs=pl.BlockSpec((group, x_local, ny), lambda i: (i, 0, 0)),
        scratch_shapes=[
            pltpu.VMEM((group, rows, ny), jnp.float32),
            pltpu.VMEM((group, chunks, rows + HALO, LANES), jnp.float32),
            pltpu.VMEM((2, chunks, rows + HALO, LANES), jnp.float32),
        ],
        compiler_params=pltpu.CompilerParams(vmem_limit_bytes=VMEM),
        name="redistance",
    )(tops, u)


def body(labels, family_of_grain, mx, my):
    parts, fams = lax.axis_size("gx"), lax.axis_size("fam")
    nz, x_local, ny = labels.shape
    assert nz == 1
    nx = x_local * parts
    fam_local = F // fams
    table = family_of_grain.reshape(-1, LANES)
    owner = gathered_owners(labels[0], table, "gx", parts, 0).reshape(nx, ny)
    u, tops = smoothed(owner, mx, my, x_local, fam_local, fams)
    return redistanced(tops, u, x_local)[:, None]


def solution(mesh):
    def run(labels, family_of_grain):
        nz, nx, ny = labels.shape
        parts = mesh.shape["gx"]
        high, low = smoothing(nx)
        rows = ring_rows(nx // parts, nx, parts)
        mx = jnp.asarray(np.concatenate([high[rows], low[rows]], axis=1))
        my = jnp.asarray(smoothing(ny)[0][None])
        mapped = jax.shard_map(
            body,
            mesh=mesh,
            in_specs=(P(None, "gx", None), P(), P(), P()),
            out_specs=P("fam", None, "gx", None),
            check_vma=False,
        )
        return mapped(labels, family_of_grain, mx, my)

    return run
```

```python
import functools

import jax
import jax.numpy as jnp
import ml_dtypes
import numpy as np
from jax import lax
from jax.experimental import pallas as pl
from jax.experimental.pallas import tpu as pltpu
from jax.sharding import PartitionSpec as P

F = 256
WIDTH = 2
SWEEPS = 3
HALO = 8
LANES = 128
BIG = -1e30
VMEM = 60 * 2**20
MESH = pl.DeviceIdType.MESH

fidelity = 0.25
scale_factor = 8.0
step_size = 0.5


def smoothing(count):
    idx = np.arange(count).astype(np.float32)
    angle = (np.float32(2.0 * np.pi) * np.outer(idx, idx)) / np.float32(count)
    cas = (np.cos(angle) + np.sin(angle)).astype(ml_dtypes.bfloat16).astype(np.float64)
    freq = np.arange(count)
    mirror = np.minimum(freq, count - freq).astype(np.float64)
    sigma = WIDTH / 2.0
    gauss = np.exp(-2.0 * np.pi**2 * sigma**2 * mirror**2 / (count * count))
    full = (cas * gauss) @ cas.T / count
    high = full.astype(ml_dtypes.bfloat16)
    low = (full - high.astype(np.float64)).astype(ml_dtypes.bfloat16)
    return high, low


def ring_rows(x_local, count, parts):
    rows = x_local + HALO
    r = np.arange(rows)
    away = np.where(r < x_local + HALO // 2, r, r - rows)
    return np.stack([(part * x_local + away) % count for part in range(parts)])


def look_up(labels_ref, table_ref, out_ref):
    rows, cols = labels_ref.shape
    words = []
    for k in range(table_ref.shape[0] // 4):
        quad = [table_ref[4 * k + b : 4 * k + b + 1, :] for b in range(4)]
        word = quad[0] + quad[1] * 2**8 + quad[2] * 2**16 + lax.shift_left(quad[3], 24)
        words.append(jnp.broadcast_to(word, (rows, LANES)))
    for c in range(cols // LANES):
        lab = labels_ref[:, c * LANES : (c + 1) * LANES]
        lane = lax.bitwise_and(lab, LANES - 1)
        page = lax.shift_right_logical(lab, LANES.bit_length() - 1)
        which = lax.shift_right_logical(page, 2)
        place = lax.bitwise_and(page, 3) * 8
        acc = jnp.take_along_axis(words[0], lane, axis=1)
        for k in range(1, len(words)):
            acc = jnp.where(which == k, jnp.take_along_axis(words[k], lane, axis=1), acc)
        acc = lax.bitwise_and(lax.shift_right_logical(acc, place), 255)
        out_ref[:, c * LANES : (c + 1) * LANES] = acc.astype(jnp.float32).astype(out_ref.dtype)


def gather_kernel(axis, size, labels_ref, table_ref, out_ref, x_ref, send_sem, recv_sem, local_sem):
    me = lax.axis_index(axis)
    chips = size // 2
    chip, core = me // 2, lax.rem(me, 2)
    beside = 2 * chip + 1 - core
    others = [2 * lax.rem(chip + d, chips) + core for d in range(1, chips)]
    barrier = pltpu.get_barrier_semaphore()
    for device in [beside, *others]:
        pl.semaphore_signal(barrier, inc=1, device_id={axis: device}, device_id_type=MESH)
    look_up(labels_ref, table_ref, x_ref)
    local = pltpu.make_async_copy(x_ref, out_ref.at[me], local_sem)
    local.start()
    pl.semaphore_wait(barrier, chips)

    def send(src, slab, device, k):
        copy = pltpu.make_async_remote_copy(
            src_ref=src,
            dst_ref=out_ref.at[slab],
            send_sem=send_sem.at[k],
            recv_sem=recv_sem.at[k],
            device_id={axis: device},
            device_id_type=MESH,
        )
        copy.start()
        return copy

    far = [send(x_ref, me, device, d) for d, device in enumerate(others)]
    near = [send(x_ref, me, beside, chips - 1)]
    for d in range(1, chips):
        far[d - 1].wait_recv()
        slab = 2 * lax.rem(chip + chips - d, chips) + core
        near.append(send(out_ref.at[slab], slab, beside, chips - 1 + d))
    local.wait()
    for copy in far:
        copy.wait_send()
    for copy in near:
        copy.wait()


def gathered_owners(labels, table, axis, size, collective_id):
    return pl.pallas_call(
        functools.partial(gather_kernel, axis, size),
        out_shape=jax.ShapeDtypeStruct((size, *labels.shape), jnp.bfloat16),
        in_specs=[pl.BlockSpec(memory_space=pltpu.VMEM)] * 2,
        out_specs=pl.BlockSpec(memory_space=pltpu.VMEM),
        scratch_shapes=[
            pltpu.VMEM(labels.shape, jnp.bfloat16),
            pltpu.SemaphoreType.DMA((size - 1,)),
            pltpu.SemaphoreType.DMA((size - 1,)),
            pltpu.SemaphoreType.DMA,
        ],
        compiler_params=pltpu.CompilerParams(
            collective_id=collective_id, has_side_effects=True, vmem_limit_bytes=VMEM
        ),
        name="gather_" + axis,
    )(labels, table)


def peers(axis, size):
    me = lax.axis_index(axis)
    return me, [lax.rem(me + k, size) for k in range(1, size)]


def greet(axis, size):
    barrier = pltpu.get_barrier_semaphore()
    for device in peers(axis, size)[1]:
        pl.semaphore_signal(barrier, inc=1, device_id={axis: device}, device_id_type=MESH)


def merge(axis, size, x_ref, out_ref, recv_ref, send_sem, recv_sem, back_send, back_recv):
    me, others = peers(axis, size)
    pl.semaphore_wait(pltpu.get_barrier_semaphore(), size - 1)

    def send(src, dst, sems, k, device):
        copy = pltpu.make_async_remote_copy(
            src_ref=src,
            dst_ref=dst,
            send_sem=sems[0].at[k],
            recv_sem=sems[1].at[k],
            device_id={axis: device},
            device_id_type=MESH,
        )
        copy.start()
        return copy

    there = [
        send(x_ref.at[device], recv_ref.at[k], (send_sem, recv_sem), k, device)
        for k, device in enumerate(others)
    ]
    high, second = x_ref[me, 0], x_ref[me, 1]
    for k in range(size - 1):
        there[k].wait_recv()
        other, third = recv_ref[k, 0], recv_ref[k, 1]
        second = jnp.maximum(jnp.minimum(high, other), jnp.maximum(second, third))
        high = jnp.maximum(high, other)
    out_ref[me, 0] = high
    out_ref[me, 1] = second
    back = [
        send(out_ref.at[me], out_ref.at[me], (back_send, back_recv), k, device)
        for k, device in enumerate(others)
    ]
    for copy in there:
        copy.wait_send()
    for copy in back:
        copy.wait()


def tile_place(k, per_piece):
    row = 8 * (k % per_piece)
    return k // per_piece, slice(row, row + 8)


def smooth_kernel(
    x_local, fam_local, group,
    owner_ref, mx_ref, my_ref, u_ref, all_ref, rel_ref, own_ref, t_ref, tops_ref, *exchange,
):
    step = pl.program_id(0)
    nx, ny = owner_ref.shape
    rows = x_local + HALO
    x0 = lax.axis_index("gx") * x_local
    first = lax.axis_index("fam") * fam_local + step * group

    @pl.when(step == 0)
    def _():
        greet("fam", tops_ref.shape[0])
        mine = owner_ref[pl.ds(pl.multiple_of(x0, x_local), x_local), :].astype(jnp.float32)
        after = lax.rem(x0 + x_local, nx)
        before = lax.rem(x0 + nx - 16, nx)
        right = owner_ref[pl.ds(pl.multiple_of(after, 16), 16), :].astype(jnp.float32)[0:HALO]
        left = owner_ref[pl.ds(pl.multiple_of(before, 16), 16), :].astype(jnp.float32)[HALO:16]
        place = lax.broadcasted_iota(jnp.int32, (HALO, ny), 0)
        own_ref[0:x_local, :] = mine
        own_ref[x_local:rows, :] = jnp.where(place < HALO // 2, right, left)
        tops_ref[...] = jnp.full(tops_ref.shape, BIG, jnp.float32)

    shift = jnp.full((nx, ny), first.astype(jnp.float32), jnp.float32).astype(jnp.bfloat16)
    rel_ref[...] = owner_ref[...] - shift
    mx = mx_ref[0]
    for j in range(group):
        chi = jnp.where(
            rel_ref[...] == jnp.bfloat16(j), jnp.bfloat16(1), jnp.bfloat16(0)
        )
        both = jnp.dot(mx, chi, preferred_element_type=jnp.float32)
        t_ref[j * rows : (j + 1) * rows, :] = both[:rows] + both[rows:]
    t = t_ref[...].astype(jnp.bfloat16)
    s = jnp.dot(t, my_ref[0], preferred_element_type=jnp.float32)
    for part in range(1, my_ref.shape[0]):
        s = s + jnp.dot(t, my_ref[part], preferred_element_type=jnp.float32)
    t_ref[...] = s
    base = first.astype(jnp.float32)
    per_piece = tops_ref.shape[2] // 8
    for r in range(rows // 8):
        strip = slice(8 * r, 8 * r + 8)
        for c in range(ny // LANES):
            cols = slice(c * LANES, (c + 1) * LANES)
            piece, place = tile_place(r * (ny // LANES) + c, per_piece)
            own = own_ref[strip, cols] - base
            high, second = tops_ref[piece, 0, place, :], tops_ref[piece, 1, place, :]
            for j in range(group):
                u = t_ref[j * rows + 8 * r : j * rows + 8 * r + 8, cols]
                u = u + jnp.where(own == float(j), fidelity, 0.0)
                u_ref[j, strip, cols] = u
                second = jnp.maximum(second, jnp.minimum(high, u))
                high = jnp.maximum(high, u)
            tops_ref[piece, 0, place, :] = high
            tops_ref[piece, 1, place, :] = second

    @pl.when(step == pl.num_programs(0) - 1)
    def _():
        merge("fam", tops_ref.shape[0], tops_ref, *exchange)
        all_ref[...] = exchange[0][...]


def smoothed(owner, mx, my, x_local, fam_local, fams):
    nx, ny = owner.shape
    rows = x_local + HALO
    group = min(8, fam_local)
    tiles = rows * ny // (8 * LANES)
    pieces = (fams, 2, 8 * (-(-tiles // fams)), LANES)
    return pl.pallas_call(
        functools.partial(smooth_kernel, x_local, fam_local, group),
        grid=(fam_local // group,),
        out_shape=(
            jax.ShapeDtypeStruct((fam_local, rows, ny), jnp.float32),
            jax.ShapeDtypeStruct(pieces, jnp.float32),
        ),
        in_specs=[
            pl.BlockSpec((nx, ny), lambda i: (0, 0)),
            pl.BlockSpec((1, *mx.shape[1:]), lambda i: (lax.axis_index("gx"), 0, 0)),
            pl.BlockSpec(my.shape, lambda i: (0, 0, 0)),
        ],
        out_specs=(
            pl.BlockSpec((group, rows, ny), lambda i: (i, 0, 0)),
            pl.BlockSpec(pieces, lambda i: (0, 0, 0, 0)),
        ),
        scratch_shapes=[
            pltpu.VMEM((nx, ny), jnp.bfloat16),
            pltpu.VMEM((rows, ny), jnp.float32),
            pltpu.VMEM((group * rows, ny), jnp.float32),
            pltpu.VMEM(pieces, jnp.float32),
            pltpu.VMEM(pieces, jnp.float32),
            pltpu.VMEM((fams - 1, *pieces[1:]), jnp.float32),
        ]
        + [pltpu.SemaphoreType.DMA((fams - 1,))] * 4,
        compiler_params=pltpu.CompilerParams(
            collective_id=1, has_side_effects=True, vmem_limit_bytes=VMEM
        ),
        name="smooth",
    )(owner, mx, my)


def redistance_kernel(x_local, group, lanes, tops_ref, u_ref, out_ref, *scratch):
    rows, ny = u_ref.shape[1:]
    chunks = ny // LANES
    strips = rows // 8

    per_piece = tops_ref.shape[2] // 8
    lane = lax.broadcasted_iota(jnp.int32, (8, LANES), 1)
    is_first, is_last = lane == 0, lane == LANES - 1

    phis = [scratch[4 * p : 4 * p + 2] for p in range(lanes)]
    sigs = [scratch[4 * p + 2] for p in range(lanes)]
    halves = [scratch[4 * p + 3] for p in range(lanes)]

    def put(ref, r, c, value):
        ref[c, 8 * r + HALO : 8 * r + HALO + 8, :] = value
        if r == strips - 1:
            ref[c, 0:HALO, :] = value

    def start(j, p):
        for r in range(strips):
            for c in range(chunks):
                rs, cs = slice(8 * r, 8 * r + 8), slice(c * LANES, (c + 1) * LANES)
                u = u_ref[j, rs, cs]
                piece, place = tile_place(r * chunks + c, per_piece)
                top1, top2 = tops_ref[piece, 0, place, :], tops_ref[piece, 1, place, :]
                phi = scale_factor * (u - jnp.where(u >= top1, top2, top1))
                put(phis[p][0], r, c, phi)
                sigs[p][c, rs, :] = jnp.where(phi > 0.0, 1.0, -1.0)
                halves[p][c, rs, :] = phi * (step_size * lax.rsqrt(phi * phi + 1.0))

    def sweep_once(j, p, sweep):
        src, dst = phis[p][sweep % 2], phis[p][(sweep + 1) % 2]
        final = sweep == SWEEPS - 1
        for r in range(x_local // 8 if final else strips):
            rs = slice(8 * r, 8 * r + 8)
            mid = [src[c, 8 * r + HALO : 8 * r + HALO + 8, :] for c in range(chunks)]
            to_right = [pltpu.roll(v, 1, 1) for v in mid]
            to_left = [pltpu.roll(v, LANES - 1, 1) for v in mid]
            for c in range(chunks):
                sig, half, centre = sigs[p][c, rs, :], halves[p][c, rs, :], mid[c]
                y_low = jnp.where(is_first, to_right[c - 1], to_right[c])
                y_high = jnp.where(is_last, to_left[(c + 1) % chunks], to_left[c])
                x_low = src[c, 8 * r + HALO - 1 : 8 * r + HALO + 7, :]
                if r == strips - 1:
                    x_high = src[c, 1:9, :]
                else:
                    x_high = src[c, 8 * r + HALO + 1 : 8 * r + HALO + 9, :]
                here = centre * sig
                gx = jnp.maximum(here - jnp.minimum(x_low * sig, x_high * sig), 1e-18)
                gy = jnp.maximum(here - jnp.minimum(y_low * sig, y_high * sig), 1e-18)
                square = gx * gx + gy * gy
                grad = square * lax.rsqrt(square)
                new = centre - half * (grad - 1.0)
                if final:
                    out_ref[j, rs, c * LANES : (c + 1) * LANES] = new
                else:
                    put(dst, r, c, new)

    def some(i, carry):
        for p in range(lanes):
            start(i * lanes + p, p)
        for sweep in range(SWEEPS):
            for p in range(lanes):
                sweep_once(i * lanes + p, p, sweep)
        return carry

    lax.fori_loop(0, group // lanes, some, 0)


def redistanced(tops, u, x_local):
    fam_local, rows, ny = u.shape
    group = min(8, fam_local)
    lanes = 4 if group % 4 == 0 else 1
    chunks = ny // LANES
    return pl.pallas_call(
        functools.partial(redistance_kernel, x_local, group, lanes),
        grid=(fam_local // group,),
        out_shape=jax.ShapeDtypeStruct((fam_local, x_local, ny), jnp.float32),
        in_specs=[
            pl.BlockSpec(tops.shape, lambda i: (0, 0, 0, 0)),
            pl.BlockSpec((group, rows, ny), lambda i: (i, 0, 0)),
        ],
        out_specs=pl.BlockSpec((group, x_local, ny), lambda i: (i, 0, 0)),
        scratch_shapes=[
            pltpu.VMEM((chunks, rows + HALO, LANES), jnp.float32),
            pltpu.VMEM((chunks, rows + HALO, LANES), jnp.float32),
            pltpu.VMEM((chunks, rows, LANES), jnp.float32),
            pltpu.VMEM((chunks, rows, LANES), jnp.float32),
        ]
        * lanes,
        compiler_params=pltpu.CompilerParams(vmem_limit_bytes=VMEM),
        name="redistance",
    )(tops, u)


def body(labels, family_of_grain, mx, my):
    parts, fams = lax.axis_size("gx"), lax.axis_size("fam")
    nz, x_local, ny = labels.shape
    assert nz == 1
    nx = x_local * parts
    fam_local = F // fams
    table = family_of_grain.reshape(-1, LANES)
    owner = gathered_owners(labels[0], table, "gx", parts, 0).reshape(nx, ny)
    u, tops = smoothed(owner, mx, my, x_local, fam_local, fams)
    return redistanced(tops, u, x_local)[:, None]


def solution(mesh):
    def run(labels, family_of_grain):
        nz, nx, ny = labels.shape
        parts = mesh.shape["gx"]
        high, low = smoothing(nx)
        rows = ring_rows(nx // parts, nx, parts)
        mx = jnp.asarray(np.concatenate([high[rows], low[rows]], axis=1))
        my = jnp.asarray(smoothing(ny)[0][None])
        mapped = jax.shard_map(
            body,
            mesh=mesh,
            in_specs=(P(None, "gx", None), P(), P(), P()),
            out_specs=P("fam", None, "gx", None),
            check_vma=False,
        )
        return mapped(labels, family_of_grain, mx, my)

    return run
```
